256 devices in a mesh: tile: 32 (over z, y), zbin: 8 (over x, core).
Axes of the slice: x: 4, y: 4, z: 8, core: 2. Of those that a mesh axis runs over, the one named last changes fastest.
Arguments:
- shear: float32 [8, 2, 1024], P('zbin', None, 'tile'), may hold values from -1.5 to 1.5
- weight: float32 [8, 1024], P('zbin', 'tile'), may hold values from 0.25 to 4
- partner_tiles: int32 [32, 4], P('tile'), may hold values from 0 to 31, as said below
- pair_count: int32 [32], P('tile'), may hold values from 1 to 4, as said below
- pair_bin: int32 [8, 8192, 128], P('zbin', 'tile'), may hold values from 0 to 24
- pair_angle: float32 [8, 8192, 128], P('zbin', 'tile'), may hold values from -3.140625 to 3.140625
Outputs:
- triples: float32 [8, 32, 73728], P('zbin', 'tile')
The draws below stay inside these ranges and needn't reach their ends.
Inputs may be any that keep to these rules, and one draw needn't show every extreme that they name: `partner_tiles`: slot 0 of each row is the tile itself; the other slots name distinct other tiles. `pair_count`: some tile uses all 4 slots and some tile only its own.
All inputs are finite; a program needn't handle non-finite values.
Results may differ from the reference program's by a relative error of at most 0.0064.
Values may be sent and summed in bfloat16 or wider, within the bound.
A program may use at most 256 MiB of HBM per device.

```python
import math
import jax
import jax.numpy as jnp
from jax import lax

GAL = 32
PMAX = 4
NM = 32
NR = 24
ZBINS = 8
TILES = 32
CEN = 256
NB = 128
KK = 36864


def draw_partner_tiles(key, part):
    key = jax.random.fold_in(key, 11)
    keys = jax.random.split(key, TILES)
    offsets = jax.vmap(lambda single: jax.random.permutation(single, TILES - 1))(keys)[:, :PMAX - 1] + 1
    own = jnp.arange(TILES, dtype=jnp.int32)[:, None]
    others = (own + offsets.astype(jnp.int32)) % TILES
    return jnp.concatenate([own, others], axis=1).astype(jnp.int32)


def draw_pair_count(key, part):
    key = jax.random.fold_in(key, 23)
    first, second, third = jax.random.split(key, 3)
    counts = jax.random.randint(first, (TILES,), 1, PMAX + 1)
    heavy = jax.random.randint(second, (), 0, TILES)
    light = (heavy + 1 + jax.random.randint(third, (), 0, TILES - 1)) % TILES
    counts = counts.at[heavy].set(PMAX)
    counts = counts.at[light].set(1)
    return counts.astype(jnp.int32)


def plant(entries, key, smallest, top_value):
    spot = [jax.random.randint(jax.random.fold_in(key, axis), (), 0, length) for axis, length in enumerate(entries.shape)]
    main_axis = entries.shape.index(max(entries.shape))
    beside = spot[:main_axis] + [(spot[main_axis] + 1) % entries.shape[main_axis]] + spot[main_axis + 1:]
    return entries.at[tuple(spot)].set(smallest).at[tuple(beside)].set(top_value)


def level_of(stream_key, extent, cuts, low, largest):
    def one(axis_at, blocks):
        heights = jax.random.uniform(jax.random.fold_in(jax.random.fold_in(stream_key, 6), axis_at), (blocks,), jnp.float32, low / len(cuts), largest / len(cuts))
        return jnp.repeat(jnp.exp(heights), extent[axis_at] // blocks).reshape((-1,) + (1,) * (len(extent) - axis_at - 1))

    level = one(*cuts[0])
    for cut in cuts[1:]:
        level = level * one(*cut)
    return level


def gaussian(own_key, dims, width, bound, cuts=(), kind=jnp.bfloat16):
    values = width * jax.random.normal(own_key, dims, jnp.float32)
    if cuts:
        values = values * level_of(own_key, dims, cuts, -0.22, 0.18)
    return jnp.clip(values, -bound, bound).astype(kind)


def setup_inputs(seed: int = 0) -> dict:
    streams_of = jax.random.split(jax.random.key(seed), 7)
    return {
        "shear": gaussian(streams_of[0], (ZBINS, 2, TILES * GAL), 0.3, 1.5, ((0, 8), (2, 32)), jnp.float32),
        "weight": jnp.clip(jnp.exp(math.log(4.0) - 2.7725887 * jax.random.uniform(streams_of[1], (ZBINS, TILES * GAL), jnp.float32) ** level_of(streams_of[1], (ZBINS, TILES * GAL), ((0, 8), (1, 32)), -0.2, 0.2)), 0.25, 4.0),
        "partner_tiles": draw_partner_tiles(jax.random.fold_in(streams_of[6], 71), 0),
        "pair_count": draw_pair_count(jax.random.fold_in(streams_of[6], 71), 0),
        "pair_bin": plant(jax.random.randint(streams_of[4], (ZBINS, TILES * CEN, NB), 0, NR + 1), jax.random.fold_in(streams_of[4], 1), 0, NR).astype(jnp.int32),
        "pair_angle": jnp.clip(jax.random.uniform(streams_of[5], (ZBINS, TILES * CEN, NB), jnp.float32, -3.140625, 3.140625), -3.140625, 3.140625),
    }


def slot_terms(angles, bins, source, live):
    orders = jnp.arange(NM).astype(jnp.float32)
    phase = angles[:, :, None] * orders[None, None, :]
    cosine = jnp.cos(phase)
    sine = jnp.sin(phase)
    first = source[0][None, :, None]
    second = source[1][None, :, None]
    scaled = (source[2] * live)[None, :, None]
    real_part = scaled * (first * cosine + second * sine)
    imag_part = scaled * (second * cosine - first * sine)
    terms = jnp.stack([real_part, imag_part], axis=2).astype(jnp.bfloat16)
    levels = jnp.arange(NR).astype(jnp.int32)
    onehot = (bins[:, :, None] == levels[None, None, :]).astype(jnp.float32)
    return jnp.einsum("ijb,ijpn->ibpn", onehot, terms.astype(jnp.float32))


def tile_tables(shear_z, weight_z, partners, count, bins, angles):
    packed = jnp.concatenate([shear_z, weight_z[None, :]], axis=0)
    total = jnp.zeros((CEN, NR, 2, NM), jnp.float32)
    for slot in range(PMAX):
        start = (partners[slot] * GAL).astype(jnp.int32)
        source = lax.dynamic_slice_in_dim(packed, start, GAL, 1)
        live = (slot < count).astype(jnp.float32)
        total = total + slot_terms(angles[:, slot * GAL:(slot + 1) * GAL], bins[:, slot * GAL:(slot + 1) * GAL], source, live)
    return total.astype(jnp.bfloat16)


def centre_sums(tables, first, second, scaled):
    grid = tables.astype(jnp.float32)
    real_in = grid[:, :, :, 0, :]
    imag_in = grid[:, :, :, 1, :]
    first = first[None, :, None, None]
    second = second[None, :, None, None]
    scaled = scaled[None, :, None, None]
    ur = (scaled * (first * real_in - second * imag_in)).astype(jnp.bfloat16).astype(jnp.float32)
    ui = (scaled * (first * imag_in + second * real_in)).astype(jnp.bfloat16).astype(jnp.float32)
    real_out = jnp.einsum("zibn,yicn->nzbyc", ur, real_in) + jnp.einsum("zibn,yicn->nzbyc", ui, imag_in)
    imag_out = jnp.einsum("zibn,yicn->nzbyc", ui, real_in) - jnp.einsum("zibn,yicn->nzbyc", ur, imag_in)
    return jnp.stack([real_out, imag_out], axis=1).reshape(NM, 2 * KK)


def reference(shear, weight, partner_tiles, pair_count, pair_bin, pair_angle):
    def tile_step(total, tile_id):
        tables = []
        for bin_id in range(ZBINS):
            rows_bin = lax.dynamic_slice_in_dim(pair_bin[bin_id], (tile_id * CEN).astype(jnp.int32), CEN, 0)
            rows_angle = lax.dynamic_slice_in_dim(pair_angle[bin_id], (tile_id * CEN).astype(jnp.int32), CEN, 0)
            tables.append(tile_tables(shear[bin_id], weight[bin_id], partner_tiles[tile_id], pair_count[tile_id], rows_bin, rows_angle))
        tables = jnp.stack(tables, axis=0)
        pieces = []
        for centre_bin in range(ZBINS):
            mine = tables[:, centre_bin * GAL:(centre_bin + 1) * GAL]
            own_shear = lax.dynamic_slice_in_dim(shear[centre_bin], (tile_id * GAL).astype(jnp.int32), GAL, 1)
            own_weight = lax.dynamic_slice_in_dim(weight[centre_bin], (tile_id * GAL).astype(jnp.int32), GAL, 0)
            pieces.append(centre_sums(mine, own_shear[0], own_shear[1], own_weight))
        return total + jnp.stack(pieces, axis=0), None

    start = jnp.zeros((ZBINS, NM, 2 * KK), jnp.float32)
    total, unused = lax.scan(tile_step, start, jnp.arange(TILES).astype(jnp.int32))
    return total * (TILES * GAL) ** -0.5
```

```python
import jax
import jax.numpy as jnp
from jax import lax
from jax.experimental import pallas as pl
from jax.experimental.pallas import tpu as pltpu
from jax.sharding import PartitionSpec as P

GAL = 32
NM = 32
NR = 24
ZB = 8
TILES = 32
YS = 4
ZS = TILES // YS
LANES = 128
HALF = 16
LEGS = ZB * NR
WIDE = 2 * LEGS
MESH = pl.DeviceIdType.MESH


def sine_cosine(phi):
    half = phi * 0.5
    sq = half * half
    sin_h = -2.5052108385e-08
    for coefficient in (2.7557319224e-06, -1.9841269841e-04, 8.3333333333e-03, -1.6666666667e-01):
        sin_h = sin_h * sq + coefficient
    sin_h = half + half * (sq * sin_h)
    cos_h = 2.0876756988e-09
    for coefficient in (-2.7557319224e-07, 2.4801587302e-05, -1.3888888889e-03, 4.1666666667e-02, -0.5):
        cos_h = cos_h * sq + coefficient
    cos_h = 1.0 + sq * cos_h
    return 2.0 * sin_h * cos_h, 1.0 - 2.0 * sin_h * sin_h


def kernel(
    shear, weight, partners, count, bins_in, angles_in, out,
    every, near, phi, bins, start, rot_c, rot_s, grid0, grid1, grid2, send, got,
    wide_re, wide_im, block_a, block_b,
    own_sem, every_send, every_recv, raw_send, raw_recv, near_send, near_recv, tab_send, tab_recv,
):
    me_t = lax.axis_index("tile")
    me_z = lax.axis_index("zbin")
    at_z, at_y = me_t // YS, me_t % YS

    def tile_at(slot):
        return ((at_z + slot // YS) % ZS) * YS + (at_y + slot % YS) % YS

    def tile_from(slot):
        return ((at_z + ZS - slot // YS) % ZS) * YS + (at_y + YS - slot % YS) % YS

    def bin_at(step):
        return (me_z + step) % ZB

    def rows_of(centre_bin):
        return pl.ds(pl.multiple_of(centre_bin * GAL, GAL), GAL)

    own_angles = pltpu.make_async_copy(angles_in.at[0, rows_of(me_z)], phi.at[me_z], own_sem.at[0])
    own_bins = pltpu.make_async_copy(bins_in.at[0, rows_of(me_z)], bins.at[me_z], own_sem.at[1])
    own_angles.start()
    own_bins.start()
    scaled = shear[0] * weight[...]
    every[0] = jnp.concatenate([scaled] * (LANES // GAL), axis=1)

    barrier = pltpu.get_barrier_semaphore()

    @pl.loop(1, TILES)
    def _(slot):
        pl.semaphore_signal(barrier, inc=1, device_id={"tile": tile_at(slot)}, device_id_type=MESH)

    @pl.loop(1, ZB)
    def _(step):
        pl.semaphore_signal(barrier, inc=1, device_id={"zbin": bin_at(step)}, device_id_type=MESH)

    pl.semaphore_wait(barrier, TILES + ZB - 2)

    def every_copy(slot):
        return pltpu.make_async_remote_copy(
            src_ref=every.at[0], dst_ref=every.at[slot],
            send_sem=every_send.at[slot], recv_sem=every_recv.at[slot],
            device_id={"tile": tile_at(slot)}, device_id_type=MESH,
        )

    def raw_copy(step, kind, source, target):
        to = bin_at(step)
        return pltpu.make_async_remote_copy(
            src_ref=source.at[0, rows_of(to)], dst_ref=target.at[me_z],
            send_sem=raw_send.at[kind, step], recv_sem=raw_recv.at[kind, step],
            device_id={"zbin": to}, device_id_type=MESH,
        )

    def near_copy(step):
        return pltpu.make_async_remote_copy(
            src_ref=near.at[me_z], dst_ref=near.at[me_z],
            send_sem=near_send.at[step], recv_sem=near_recv.at[step],
            device_id={"zbin": bin_at(step)}, device_id_type=MESH,
        )

    @pl.loop(1, TILES)
    def _(slot):
        every_copy(slot).start()

    @pl.loop(1, ZB)
    def _(step):
        raw_copy(step, 0, angles_in, phi).start()
        raw_copy(step, 1, bins_in, bins).start()

    own_angles.wait()
    own_bins.wait()

    @pl.loop(1, TILES)
    def _(slot):
        every_copy(slot).wait_recv()

    lane = lax.broadcasted_iota(jnp.int32, (2, LANES), 1)
    place = lane // GAL
    wanted = jnp.full((2, LANES), partners[0, 0])
    for slot in range(1, LANES // GAL):
        wanted = jnp.where(place == slot, partners[0, slot], wanted)
    wanted = jnp.where(place < count[0], wanted, -1)
    picked = jnp.zeros((2, LANES), jnp.float32)
    for slot in range(TILES):
        picked = picked + jnp.where(wanted == tile_from(slot), every[slot], 0.0)
    near[me_z] = picked

    @pl.loop(1, ZB)
    def _(step):
        near_copy(step).start()

    @pl.loop(1, ZB)
    def _(step):
        raw_copy(step, 0, angles_in, phi).wait_recv()
        raw_copy(step, 1, bins_in, bins).wait_recv()

    @pl.loop(0, ZB)
    def _(z):
        sine, cosine = sine_cosine(phi[z])
        phi[z] = cosine
        rot_s[z] = sine

    @pl.loop(1, ZB)
    def _(step):
        near_copy(step).wait_recv()

    @pl.loop(0, ZB)
    def _(z):
        cosine, sine = phi[z], rot_s[z]
        first = jnp.broadcast_to(near[z, 0:1, :], (GAL, LANES))
        second = jnp.broadcast_to(near[z, 1:2, :], (GAL, LANES))
        twice = 2.0 * cosine
        base = pl.multiple_of(z * 16 * GAL, 16 * GAL)
        old_re, old_im = first, second
        new_re = first * cosine + second * sine
        new_im = second * cosine - first * sine
        for n in range(8):
            start[pl.ds(base + n * GAL, GAL), :] = old_re
            start[pl.ds(base + (8 + n) * GAL, GAL), :] = old_im
            old_re, new_re = new_re, twice * new_re - old_re
            old_im, new_im = new_im, twice * new_im - old_im
        for _ in range(3):
            cosine, sine = 1.0 - 2.0 * sine * sine, 2.0 * sine * cosine
        rot_c[z] = cosine
        rot_s[z] = sine

    level = lax.broadcasted_iota(jnp.int32, (NR, LANES), 0)
    blank = jnp.zeros((NR, LANES), jnp.float32)

    def centre_table(i, local):
        parts = []
        for pair in range(ZB // 2):
            terms, hits = [], []
            for z in (2 * pair, 2 * pair + 1):
                base = z * 16 * GAL
                re = [start[pl.ds(base + i, 8, stride=GAL), :]]
                im = [start[pl.ds(base + 8 * GAL + i, 8, stride=GAL), :]]
                cosine = jnp.broadcast_to(rot_c[z, pl.ds(i, 1), :], (8, LANES))
                sine = jnp.broadcast_to(rot_s[z, pl.ds(i, 1), :], (8, LANES))
                twice = cosine + cosine
                re.append(re[0] * cosine + im[0] * sine)
                im.append(im[0] * cosine - re[0] * sine)
                for _ in range(2):
                    re.append(twice * re[-1] - re[-2])
                    im.append(twice * im[-1] - im[-2])
                terms.append(jnp.concatenate(re + im, axis=0).astype(jnp.bfloat16))
                row = jnp.broadcast_to(bins[z, pl.ds(i, 1), :], (NR, LANES))
                hits.append(jnp.where(row == level, 1.0, 0.0))
            onehot = jnp.concatenate(
                [jnp.concatenate([hits[0], blank], axis=1), jnp.concatenate([blank, hits[1]], axis=1)],
                axis=0,
            ).astype(jnp.bfloat16)
            parts.append(
                lax.dot_general(
                    jnp.concatenate(terms, axis=1), onehot, (((1,), (1,)), ((), ())),
                    preferred_element_type=jnp.float32,
                )
            )
        table = jnp.concatenate(parts, axis=1)
        rows = pl.ds(local, NM, stride=HALF)
        grid0[rows, :] = table[:NM, :LANES]
        grid1[rows, :] = jnp.concatenate([table[:NM, LANES:], table[NM:, LANES:]], axis=1)
        grid2[rows, :] = table[NM:, :LANES]

    def table_copy(half, slot):
        return pltpu.make_async_remote_copy(
            src_ref=send.at[half, tile_at(slot)],
            dst_ref=got.at[pl.ds(pl.multiple_of(slot * GAL + half * HALF, HALF), HALF), :],
            send_sem=tab_send.at[half, slot], recv_sem=tab_recv.at[half, slot],
            device_id={"tile": tile_at(slot)}, device_id_type=MESH,
        )

    for half in range(2):
        @pl.loop(0, HALF, unroll=2)
        def _(local):
            centre_table(half * HALF + local, local)

        @pl.loop(0, NM, unroll=4)
        def _(n):
            rows = pl.ds(pl.multiple_of(n * HALF, HALF), HALF)
            send[half, n, :, 0:LANES] = grid0[rows, :].astype(jnp.bfloat16)
            send[half, n, :, LANES:2 * LANES] = grid1[rows, :].astype(jnp.bfloat16)
            send[half, n, :, 2 * LANES:] = grid2[rows, :].astype(jnp.bfloat16)

        @pl.loop(1, TILES)
        def _(slot):
            table_copy(half, slot).start()

        got[half * HALF:(half + 1) * HALF, :] = send[half, me_t]

    lane = lax.broadcasted_iota(jnp.int32, (2, LANES), 1)
    wide_re[...] = jnp.zeros_like(wide_re)
    wide_im[...] = jnp.zeros_like(wide_im)
    group = 8
    for g in range(TILES // group):
        @pl.loop(max(g * group, 1), (g + 1) * group)
        def _(slot):
            for half in range(2):
                table_copy(half, slot).wait_recv()

        block = got[g * group * GAL:(g + 1) * group * GAL, :]
        turned = block.T.astype(jnp.float32)
        scales = []
        for quad in range(group * GAL // LANES):
            first = g * group + quad * (LANES // GAL)
            row = every[first]
            for k in range(1, LANES // GAL):
                row = jnp.where(lane // GAL == k, every[first + k], row)
            scales.append(row)
        scales = jnp.concatenate(scales, axis=1)
        first, second = scales[0:1], scales[1:2]
        real_in = turned[:LEGS]
        imag_in = jnp.concatenate([turned[WIDE - LANES:], turned[LEGS:WIDE - LANES]], axis=0)
        upper_re = (first * real_in - second * imag_in).astype(jnp.bfloat16)
        upper_im = (first * imag_in + second * real_in).astype(jnp.bfloat16)
        wide_re[...] += jnp.dot(upper_re, block, preferred_element_type=jnp.float32)
        wide_im[...] += jnp.dot(upper_im, block, preferred_element_type=jnp.float32)

    scale = float(TILES * GAL) ** -0.5
    low = lax.broadcasted_iota(jnp.int32, (LEGS // 2, LANES), 1) < LANES // 2
    for part in range(2):
        if part == 0:
            whole = wide_re[:, :LANES] + wide_im[:, 2 * LANES:]
            rest = wide_re[:, LANES:2 * LANES] + pltpu.roll(wide_im[:, LANES:2 * LANES], LANES // 2, 1)
        else:
            whole = wide_im[:, :LANES] - wide_re[:, 2 * LANES:]
            rest = wide_im[:, LANES:2 * LANES] - pltpu.roll(wide_re[:, LANES:2 * LANES], LANES // 2, 1)
        block_a[...] = whole * scale
        block_b[...] = rest * scale
        base = part * LEGS * LEGS // LANES
        even_a = block_a[pl.ds(0, LEGS // 2, stride=2), :]
        odd_a = pltpu.roll(block_a[pl.ds(1, LEGS // 2, stride=2), :], LANES // 2, 1)
        even_b = block_b[pl.ds(0, LEGS // 2, stride=2), :]
        odd_b = pltpu.roll(block_b[pl.ds(1, LEGS // 2, stride=2), :], LANES // 2, 1)
        out[pl.ds(base, LEGS // 2, stride=3), :] = even_a
        out[pl.ds(base + 1, LEGS // 2, stride=3), :] = jnp.where(low, even_b, odd_a)
        out[pl.ds(base + 2, LEGS // 2, stride=3), :] = jnp.where(low, odd_a, odd_b)

    @pl.loop(1, TILES)
    def _(slot):
        every_copy(slot).wait_send()
        for half in range(2):
            table_copy(half, slot).wait_send()

    @pl.loop(1, ZB)
    def _(step):
        raw_copy(step, 0, angles_in, phi).wait_send()
        raw_copy(step, 1, bins_in, bins).wait_send()
        near_copy(step).wait_send()


def per_device(shear, weight, partner_tiles, pair_count, pair_bin, pair_angle):
    vmem = pl.BlockSpec(memory_space=pltpu.VMEM)
    smem = pl.BlockSpec(memory_space=pltpu.SMEM)
    anywhere = pl.BlockSpec(memory_space=pl.ANY)
    f32, bf16 = jnp.float32, jnp.bfloat16
    flat = pl.pallas_call(
        kernel,
        out_shape=jax.ShapeDtypeStruct((2 * LEGS * LEGS // LANES, LANES), f32),
        in_specs=[vmem, vmem, smem, smem, anywhere, anywhere],
        out_specs=vmem,
        scratch_shapes=[
            pltpu.VMEM((TILES, 2, LANES), f32),
            pltpu.VMEM((ZB, 2, LANES), f32),
            pltpu.VMEM((ZB, GAL, LANES), f32),
            pltpu.VMEM((ZB, GAL, LANES), jnp.int32),
            pltpu.VMEM((ZB * 16 * GAL, LANES), f32),
            pltpu.VMEM((ZB, GAL, LANES), f32),
            pltpu.VMEM((ZB, GAL, LANES), f32),
            pltpu.VMEM((NM * HALF, LANES), f32),
            pltpu.VMEM((NM * HALF, LANES), f32),
            pltpu.VMEM((NM * HALF, LANES), f32),
            pltpu.VMEM((2, NM, HALF, WIDE), bf16),
            pltpu.VMEM((TILES * GAL, WIDE), bf16),
            pltpu.VMEM((LEGS, WIDE), f32),
            pltpu.VMEM((LEGS, WIDE), f32),
            pltpu.VMEM((LEGS, LANES), f32),
            pltpu.VMEM((LEGS, LANES), f32),
            pltpu.SemaphoreType.DMA((2,)),
            pltpu.SemaphoreType.DMA((TILES,)),
            pltpu.SemaphoreType.DMA((TILES,)),
            pltpu.SemaphoreType.DMA((2, ZB)),
            pltpu.SemaphoreType.DMA((2, ZB)),
            pltpu.SemaphoreType.DMA((ZB,)),
            pltpu.SemaphoreType.DMA((ZB,)),
            pltpu.SemaphoreType.DMA((2, TILES)),
            pltpu.SemaphoreType.DMA((2, TILES)),
        ],
        compiler_params=pltpu.CompilerParams(
            collective_id=0, has_side_effects=True, vmem_limit_bytes=40 * 1024 * 1024
        ),
        cost_estimate=pl.CostEstimate(flops=800_000_000, bytes_accessed=2_000_000, transcendentals=0),
        name="shear_triples",
    )(shear, weight, partner_tiles, pair_count, pair_bin, pair_angle)
    return flat.reshape(1, 1, 2 * LEGS * LEGS)


def solution(mesh):
    return jax.shard_map(
        per_device,
        mesh=mesh,
        in_specs=(
            P("zbin", None, "tile"),
            P("zbin", "tile"),
            P("tile", None),
            P("tile"),
            P("zbin", "tile", None),
            P("zbin", "tile", None),
        ),
        out_specs=P("zbin", "tile", None),
        check_vma=False,
    )
```

```python
import jax
import jax.numpy as jnp
from jax import lax
from jax.experimental import pallas as pl
from jax.experimental.pallas import tpu as pltpu
from jax.sharding import PartitionSpec as P

GAL = 32
NM = 32
NR = 24
ZB = 8
TILES = 32
YS = 4
ZS = TILES // YS
LANES = 128
HALF = 16
LEGS = ZB * NR
WIDE = 2 * LEGS
OWN = TILES - 1
MESH = pl.DeviceIdType.MESH


def sine_cosine(phi):
    half = phi * 0.5
    sq = half * half
    sin_h = -2.5052108385e-08
    for coefficient in (2.7557319224e-06, -1.9841269841e-04, 8.3333333333e-03, -1.6666666667e-01):
        sin_h = sin_h * sq + coefficient
    sin_h = half + half * (sq * sin_h)
    cos_h = 2.0876756988e-09
    for coefficient in (-2.7557319224e-07, 2.4801587302e-05, -1.3888888889e-03, 4.1666666667e-02, -0.5):
        cos_h = cos_h * sq + coefficient
    cos_h = 1.0 + sq * cos_h
    return 2.0 * sin_h * cos_h, 1.0 - 2.0 * sin_h * sin_h


def kernel(
    shear_in, weight_in, partners_in, count_in, bins_in, angles_in, out,
    shear, weight, partners, count, every, near, phi, bins, start, rot_c, rot_s, grid0, grid1, grid2, send, got,
    wide_re, wide_im, block_a, block_b,
    small_sem, own_sem, every_send, every_recv, raw_send, raw_recv, near_send, near_recv, tab_send, tab_recv,
):
    me_t = lax.axis_index("tile")
    me_z = lax.axis_index("zbin")
    at_z, at_y = me_t // YS, me_t % YS

    def steps(slot):
        k = slot // YS
        return (ZS // 2 + (k + 1) // 2 * (1 - 2 * (k % 2))) % ZS, (slot + 1) % YS

    def tile_at(slot):
        z, y = steps(slot)
        return ((at_z + z) % ZS) * YS + (at_y + y) % YS

    def tile_from(slot):
        z, y = steps(slot)
        return ((at_z + ZS - z) % ZS) * YS + (at_y + YS - y) % YS

    def bin_at(step):
        return (me_z + step) % ZB

    def rows_of(centre_bin):
        return pl.ds(pl.multiple_of(centre_bin * GAL, GAL), GAL)

    small = [
        pltpu.make_async_copy(shear_in, shear, small_sem.at[0]),
        pltpu.make_async_copy(weight_in, weight, small_sem.at[1]),
        pltpu.make_async_copy(partners_in, partners, small_sem.at[2]),
        pltpu.make_async_copy(count_in, count, small_sem.at[3]),
    ]
    for copy in small:
        copy.start()
    own_angles = pltpu.make_async_copy(angles_in.at[0, rows_of(me_z)], phi.at[me_z], own_sem.at[0])
    own_bins = pltpu.make_async_copy(bins_in.at[0, rows_of(me_z)], bins.at[me_z], own_sem.at[1])
    own_angles.start()
    own_bins.start()
    barrier = pltpu.get_barrier_semaphore()

    @pl.loop(0, OWN)
    def _(slot):
        pl.semaphore_signal(barrier, inc=1, device_id={"tile": tile_at(slot)}, device_id_type=MESH)

    @pl.loop(1, ZB)
    def _(step):
        pl.semaphore_signal(barrier, inc=1, device_id={"zbin": bin_at(step)}, device_id_type=MESH)

    for copy in small:
        copy.wait()
    scaled = shear[0] * weight[...]
    every[OWN] = jnp.concatenate([scaled] * (LANES // GAL), axis=1)
    pl.semaphore_wait(barrier, TILES + ZB - 2)

    def every_copy(slot):
        return pltpu.make_async_remote_copy(
            src_ref=every.at[OWN], dst_ref=every.at[slot],
            send_sem=every_send.at[slot], recv_sem=every_recv.at[slot],
            device_id={"tile": tile_at(slot)}, device_id_type=MESH,
        )

    def raw_copy(step, kind, source, target):
        to = bin_at(step)
        return pltpu.make_async_remote_copy(
            src_ref=source.at[0, rows_of(to)], dst_ref=target.at[me_z],
            send_sem=raw_send.at[kind, step], recv_sem=raw_recv.at[kind, step],
            device_id={"zbin": to}, device_id_type=MESH,
        )

    def near_copy(step):
        return pltpu.make_async_remote_copy(
            src_ref=near.at[me_z], dst_ref=near.at[me_z],
            send_sem=near_send.at[step], recv_sem=near_recv.at[step],
            device_id={"zbin": bin_at(step)}, device_id_type=MESH,
        )

    @pl.loop(0, OWN)
    def _(slot):
        every_copy(slot).start()

    @pl.loop(1, ZB)
    def _(step):
        raw_copy(step, 0, angles_in, phi).start()
        raw_copy(step, 1, bins_in, bins).start()

    own_angles.wait()
    own_bins.wait()

    @pl.loop(0, OWN)
    def _(slot):
        every_copy(slot).wait_recv()

    lane = lax.broadcasted_iota(jnp.int32, (2, LANES), 1)
    place = lane // GAL
    wanted = jnp.full((2, LANES), partners[0, 0])
    for slot in range(1, LANES // GAL):
        wanted = jnp.where(place == slot, partners[0, slot], wanted)
    wanted = jnp.where(place < count[0, 0], wanted, -1)
    picked = jnp.zeros((2, LANES), jnp.float32)
    for slot in range(TILES):
        picked = picked + jnp.where(wanted == tile_from(slot), every[slot], 0.0)
    near[me_z] = picked

    @pl.loop(1, ZB)
    def _(step):
        near_copy(step).start()

    @pl.loop(1, ZB)
    def _(step):
        raw_copy(step, 0, angles_in, phi).wait_recv()
        raw_copy(step, 1, bins_in, bins).wait_recv()

    @pl.loop(0, ZB)
    def _(z):
        sine, cosine = sine_cosine(phi[z])
        phi[z] = cosine
        rot_s[z] = sine

    @pl.loop(1, ZB)
    def _(step):
        near_copy(step).wait_recv()

    @pl.loop(0, ZB)
    def _(z):
        cosine, sine = phi[z], rot_s[z]
        first = jnp.broadcast_to(near[z, 0:1, :], (GAL, LANES))
        second = jnp.broadcast_to(near[z, 1:2, :], (GAL, LANES))
        twice = 2.0 * cosine
        base = pl.multiple_of(z * 16 * GAL, 16 * GAL)
        old_re, old_im = first, second
        new_re = first * cosine + second * sine
        new_im = second * cosine - first * sine
        for n in range(8):
            start[pl.ds(base + n * GAL, GAL), :] = old_re
            start[pl.ds(base + (8 + n) * GAL, GAL), :] = old_im
            old_re, new_re = new_re, twice * new_re - old_re
            old_im, new_im = new_im, twice * new_im - old_im
        for _ in range(3):
            cosine, sine = 1.0 - 2.0 * sine * sine, 2.0 * sine * cosine
        rot_c[z] = cosine
        rot_s[z] = sine

    level = lax.broadcasted_iota(jnp.int32, (NR, LANES), 0)
    blank = jnp.zeros((NR, LANES), jnp.float32)

    def centre_table(i, local):
        parts = []
        for pair in range(ZB // 2):
            terms, hits = [], []
            for z in (2 * pair, 2 * pair + 1):
                base = z * 16 * GAL
                re = [start[pl.ds(base + i, 8, stride=GAL), :]]
                im = [start[pl.ds(base + 8 * GAL + i, 8, stride=GAL), :]]
                cosine = jnp.broadcast_to(rot_c[z, pl.ds(i, 1), :], (8, LANES))
                sine = jnp.broadcast_to(rot_s[z, pl.ds(i, 1), :], (8, LANES))
                twice = cosine + cosine
                re.append(re[0] * cosine + im[0] * sine)
                im.append(im[0] * cosine - re[0] * sine)
                for _ in range(2):
                    re.append(twice * re[-1] - re[-2])
                    im.append(twice * im[-1] - im[-2])
                terms.append(jnp.concatenate(re + im, axis=0).astype(jnp.bfloat16))
                row = jnp.broadcast_to(bins[z, pl.ds(i, 1), :], (NR, LANES))
                hits.append(jnp.where(row == level, 1.0, 0.0))
            onehot = jnp.concatenate(
                [jnp.concatenate([hits[0], blank], axis=1), jnp.concatenate([blank, hits[1]], axis=1)],
                axis=0,
            ).astype(jnp.bfloat16)
            parts.append(
                lax.dot_general(
                    jnp.concatenate(terms, axis=1), onehot, (((1,), (1,)), ((), ())),
                    preferred_element_type=jnp.float32,
                )
            )
        table = jnp.concatenate(parts, axis=1)
        rows = pl.ds(local, NM, stride=HALF)
        grid0[rows, :] = table[:NM, :LANES]
        grid1[rows, :] = jnp.concatenate([table[:NM, LANES:], table[NM:, LANES:]], axis=1)
        grid2[rows, :] = table[NM:, :LANES]

    def table_copy(half, slot):
        return pltpu.make_async_remote_copy(
            src_ref=send.at[half, tile_at(slot)],
            dst_ref=got.at[pl.ds(pl.multiple_of(slot * GAL + half * HALF, HALF), HALF), :],
            send_sem=tab_send.at[half, slot], recv_sem=tab_recv.at[half, slot],
            device_id={"tile": tile_at(slot)}, device_id_type=MESH,
        )

    for half in range(2):
        @pl.loop(0, HALF, unroll=2)
        def _(local):
            centre_table(half * HALF + local, local)

        @pl.loop(0, NM, unroll=4)
        def _(n):
            rows = pl.ds(pl.multiple_of(n * HALF, HALF), HALF)
            send[half, n, :, 0:LANES] = grid0[rows, :].astype(jnp.bfloat16)
            send[half, n, :, LANES:2 * LANES] = grid1[rows, :].astype(jnp.bfloat16)
            send[half, n, :, 2 * LANES:] = grid2[rows, :].astype(jnp.bfloat16)

        @pl.loop(0, OWN)
        def _(slot):
            table_copy(half, slot).start()

        got[OWN * GAL + half * HALF:OWN * GAL + (half + 1) * HALF, :] = send[half, me_t]

    lane = lax.broadcasted_iota(jnp.int32, (2, LANES), 1)
    wide_re[...] = jnp.zeros_like(wide_re)
    wide_im[...] = jnp.zeros_like(wide_im)
    group = 8
    for g in range(TILES // group):
        @pl.loop(g * group, min((g + 1) * group, OWN))
        def _(slot):
            for half in range(2):
                table_copy(half, slot).wait_recv()

        block = got[g * group * GAL:(g + 1) * group * GAL, :]
        turned = block.T.astype(jnp.float32)
        scales = []
        for quad in range(group * GAL // LANES):
            first = g * group + quad * (LANES // GAL)
            row = every[first]
            for k in range(1, LANES // GAL):
                row = jnp.where(lane // GAL == k, every[first + k], row)
            scales.append(row)
        scales = jnp.concatenate(scales, axis=1)
        first, second = scales[0:1], scales[1:2]
        real_in = turned[:LEGS]
        imag_in = jnp.concatenate([turned[WIDE - LANES:], turned[LEGS:WIDE - LANES]], axis=0)
        upper_re = (first * real_in - second * imag_in).astype(jnp.bfloat16)
        upper_im = (first * imag_in + second * real_in).astype(jnp.bfloat16)
        wide_re[...] += jnp.dot(upper_re, block, preferred_element_type=jnp.float32)
        wide_im[...] += jnp.dot(upper_im, block, preferred_element_type=jnp.float32)

    scale = float(TILES * GAL) ** -0.5
    low = lax.broadcasted_iota(jnp.int32, (LEGS // 2, LANES), 1) < LANES // 2
    for part in range(2):
        if part == 0:
            whole = wide_re[:, :LANES] + wide_im[:, 2 * LANES:]
            rest = wide_re[:, LANES:2 * LANES] + pltpu.roll(wide_im[:, LANES:2 * LANES], LANES // 2, 1)
        else:
            whole = wide_im[:, :LANES] - wide_re[:, 2 * LANES:]
            rest = wide_im[:, LANES:2 * LANES] - pltpu.roll(wide_re[:, LANES:2 * LANES], LANES // 2, 1)
        block_a[...] = whole * scale
        block_b[...] = rest * scale
        base = part * LEGS * LEGS // LANES
        even_a = block_a[pl.ds(0, LEGS // 2, stride=2), :]
        odd_a = pltpu.roll(block_a[pl.ds(1, LEGS // 2, stride=2), :], LANES // 2, 1)
        even_b = block_b[pl.ds(0, LEGS // 2, stride=2), :]
        odd_b = pltpu.roll(block_b[pl.ds(1, LEGS // 2, stride=2), :], LANES // 2, 1)
        out[pl.ds(base, LEGS // 2, stride=3), :] = even_a
        out[pl.ds(base + 1, LEGS // 2, stride=3), :] = jnp.where(low, even_b, odd_a)
        out[pl.ds(base + 2, LEGS // 2, stride=3), :] = jnp.where(low, odd_a, odd_b)

    @pl.loop(0, OWN)
    def _(slot):
        every_copy(slot).wait_send()
        for half in range(2):
            table_copy(half, slot).wait_send()

    @pl.loop(1, ZB)
    def _(step):
        raw_copy(step, 0, angles_in, phi).wait_send()
        raw_copy(step, 1, bins_in, bins).wait_send()
        near_copy(step).wait_send()


def per_device(shear, weight, partner_tiles, pair_count, pair_bin, pair_angle):
    vmem = pl.BlockSpec(memory_space=pltpu.VMEM)
    anywhere = pl.BlockSpec(memory_space=pl.ANY)
    f32, bf16 = jnp.float32, jnp.bfloat16
    flat = pl.pallas_call(
        kernel,
        out_shape=pltpu.VMEM((2 * LEGS * LEGS // LANES, LANES), f32),
        in_specs=[anywhere] * 6,
        out_specs=vmem,
        scratch_shapes=[
            pltpu.VMEM((1, 2, GAL), f32),
            pltpu.VMEM((1, GAL), f32),
            pltpu.SMEM((1, LANES // GAL), jnp.int32),
            pltpu.SMEM((1, 1), jnp.int32),
            pltpu.VMEM((TILES, 2, LANES), f32),
            pltpu.VMEM((ZB, 2, LANES), f32),
            pltpu.VMEM((ZB, GAL, LANES), f32),
            pltpu.VMEM((ZB, GAL, LANES), jnp.int32),
            pltpu.VMEM((ZB * 16 * GAL, LANES), f32),
            pltpu.VMEM((ZB, GAL, LANES), f32),
            pltpu.VMEM((ZB, GAL, LANES), f32),
            pltpu.VMEM((NM * HALF, LANES), f32),
            pltpu.VMEM((NM * HALF, LANES), f32),
            pltpu.VMEM((NM * HALF, LANES), f32),
            pltpu.VMEM((2, NM, HALF, WIDE), bf16),
            pltpu.VMEM((TILES * GAL, WIDE), bf16),
            pltpu.VMEM((LEGS, WIDE), f32),
            pltpu.VMEM((LEGS, WIDE), f32),
            pltpu.VMEM((LEGS, LANES), f32),
            pltpu.VMEM((LEGS, LANES), f32),
            pltpu.SemaphoreType.DMA((4,)),
            pltpu.SemaphoreType.DMA((2,)),
            pltpu.SemaphoreType.DMA((TILES,)),
            pltpu.SemaphoreType.DMA((TILES,)),
            pltpu.SemaphoreType.DMA((2, ZB)),
            pltpu.SemaphoreType.DMA((2, ZB)),
            pltpu.SemaphoreType.DMA((ZB,)),
            pltpu.SemaphoreType.DMA((ZB,)),
            pltpu.SemaphoreType.DMA((2, TILES)),
            pltpu.SemaphoreType.DMA((2, TILES)),
        ],
        compiler_params=pltpu.CompilerParams(
            collective_id=0, has_side_effects=True, vmem_limit_bytes=60 * 1024 * 1024
        ),
        cost_estimate=pl.CostEstimate(flops=800_000_000, bytes_accessed=2_000_000, transcendentals=0),
        name="shear_triples",
    )(shear, weight, partner_tiles, pair_count.reshape(1, 1), pair_bin, pair_angle)
    return flat.reshape(1, 1, 2 * LEGS * LEGS)


def solution(mesh):
    return jax.shard_map(
        per_device,
        mesh=mesh,
        in_specs=(
            P("zbin", None, "tile"),
            P("zbin", "tile"),
            P("tile", None),
            P("tile"),
            P("zbin", "tile", None),
            P("zbin", "tile", None),
        ),
        out_specs=P("zbin", "tile", None),
        check_vma=False,
    )
```

```python
import jax
import jax.numpy as jnp
from jax import lax
from jax.experimental import pallas as pl
from jax.experimental.pallas import tpu as pltpu
from jax.sharding import PartitionSpec as P

GAL = 32
NM = 32
NR = 24
ZB = 8
TILES = 32
YS = 4
ZS = TILES // YS
LANES = 128
HALF = 16
LEGS = ZB * NR
WIDE = 2 * LEGS
OWN = TILES - 1
MESH = pl.DeviceIdType.MESH


def sine_cosine(phi):
    half = phi * 0.5
    sq = half * half
    sin_h = -2.5052108385e-08
    for coefficient in (2.7557319224e-06, -1.9841269841e-04, 8.3333333333e-03, -1.6666666667e-01):
        sin_h = sin_h * sq + coefficient
    sin_h = half + half * (sq * sin_h)
    cos_h = 2.0876756988e-09
    for coefficient in (-2.7557319224e-07, 2.4801587302e-05, -1.3888888889e-03, 4.1666666667e-02, -0.5):
        cos_h = cos_h * sq + coefficient
    cos_h = 1.0 + sq * cos_h
    return 2.0 * sin_h * cos_h, 1.0 - 2.0 * sin_h * sin_h


def kernel(
    shear_in, weight_in, partners_in, count_in, bins_in, angles_in, out,
    shear, weight, partners, count, every, near, phi, bins, start, rot_c, rot_s, grid0, grid1, grid2, send, got,
    wide_re, wide_im, block_a, block_b,
    small_sem, own_sem, every_send, every_recv, raw_send, raw_recv, near_send, near_recv, tab_send, tab_recv,
):
    me_t = lax.axis_index("tile")
    me_z = lax.axis_index("zbin")
    at_z, at_y = me_t // YS, me_t % YS

    def steps(slot):
        k = slot // YS
        return (ZS // 2 + (k + 1) // 2 * (1 - 2 * (k % 2))) % ZS, (slot + 1) % YS

    def tile_at(slot):
        z, y = steps(slot)
        return ((at_z + z) % ZS) * YS + (at_y + y) % YS

    def tile_from(slot):
        z, y = steps(slot)
        return ((at_z + ZS - z) % ZS) * YS + (at_y + YS - y) % YS

    def bin_at(step):
        return (me_z + step) % ZB

    def rows_of(centre_bin):
        return pl.ds(pl.multiple_of(centre_bin * GAL, GAL), GAL)

    small = [
        pltpu.make_async_copy(shear_in, shear, small_sem.at[0]),
        pltpu.make_async_copy(weight_in, weight, small_sem.at[1]),
        pltpu.make_async_copy(partners_in, partners, small_sem.at[2]),
        pltpu.make_async_copy(count_in, count, small_sem.at[3]),
    ]
    for copy in small:
        copy.start()
    own_angles = pltpu.make_async_copy(angles_in.at[0, rows_of(me_z)], phi.at[me_z], own_sem.at[0])
    own_bins = pltpu.make_async_copy(bins_in.at[0, rows_of(me_z)], bins.at[me_z], own_sem.at[1])
    own_angles.start()
    own_bins.start()
    barrier = pltpu.get_barrier_semaphore()

    @pl.loop(0, OWN)
    def _(slot):
        pl.semaphore_signal(barrier, inc=1, device_id={"tile": tile_at(slot)}, device_id_type=MESH)

    @pl.loop(1, ZB)
    def _(step):
        pl.semaphore_signal(barrier, inc=1, device_id={"zbin": bin_at(step)}, device_id_type=MESH)

    for copy in small:
        copy.wait()
    scaled = shear[0] * weight[...]
    every[OWN] = jnp.concatenate([scaled] * (LANES // GAL), axis=1)
    pl.semaphore_wait(barrier, TILES + ZB - 2)

    def every_copy(slot):
        return pltpu.make_async_remote_copy(
            src_ref=every.at[OWN], dst_ref=every.at[slot],
            send_sem=every_send.at[slot], recv_sem=every_recv.at[slot],
            device_id={"tile": tile_at(slot)}, device_id_type=MESH,
        )

    def raw_copy(step, kind, source, target):
        to = bin_at(step)
        return pltpu.make_async_remote_copy(
            src_ref=source.at[0, rows_of(to)], dst_ref=target.at[me_z],
            send_sem=raw_send.at[kind, step], recv_sem=raw_recv.at[kind, step],
            device_id={"zbin": to}, device_id_type=MESH,
        )

    def near_copy(step):
        return pltpu.make_async_remote_copy(
            src_ref=near.at[me_z], dst_ref=near.at[me_z],
            send_sem=near_send.at[step], recv_sem=near_recv.at[step],
            device_id={"zbin": bin_at(step)}, device_id_type=MESH,
        )

    @pl.loop(0, OWN)
    def _(slot):
        every_copy(slot).start()

    @pl.loop(1, ZB)
    def _(step):
        raw_copy(step, 0, angles_in, phi).start()
        raw_copy(step, 1, bins_in, bins).start()

    own_angles.wait()
    own_bins.wait()

    @pl.loop(0, OWN)
    def _(slot):
        every_copy(slot).wait_recv()

    lane = lax.broadcasted_iota(jnp.int32, (2, LANES), 1)
    place = lane // GAL
    wanted = jnp.full((2, LANES), partners[0, 0])
    for slot in range(1, LANES // GAL):
        wanted = jnp.where(place == slot, partners[0, slot], wanted)
    wanted = jnp.where(place < count[0, 0], wanted, -1)
    picked = jnp.zeros((2, LANES), jnp.float32)
    for slot in range(TILES):
        picked = picked + jnp.where(wanted == tile_from(slot), every[slot], 0.0)
    near[me_z] = picked

    @pl.loop(1, ZB)
    def _(step):
        near_copy(step).start()

    @pl.loop(1, ZB)
    def _(step):
        raw_copy(step, 0, angles_in, phi).wait_recv()
        raw_copy(step, 1, bins_in, bins).wait_recv()

    @pl.loop(0, ZB)
    def _(z):
        sine, cosine = sine_cosine(phi[z])
        phi[z] = cosine
        rot_s[z] = sine

    @pl.loop(1, ZB)
    def _(step):
        near_copy(step).wait_recv()

    @pl.loop(0, ZB)
    def _(z):
        cosine, sine = phi[z], rot_s[z]
        first = jnp.broadcast_to(near[z, 0:1, :], (GAL, LANES))
        second = jnp.broadcast_to(near[z, 1:2, :], (GAL, LANES))
        twice = 2.0 * cosine
        base = pl.multiple_of(z * 16 * GAL, 16 * GAL)
        old_re, old_im = first, second
        new_re = first * cosine + second * sine
        new_im = second * cosine - first * sine
        for n in range(8):
            start[pl.ds(base + n * GAL, GAL), :] = old_re
            start[pl.ds(base + (8 + n) * GAL, GAL), :] = old_im
            old_re, new_re = new_re, twice * new_re - old_re
            old_im, new_im = new_im, twice * new_im - old_im
        for _ in range(3):
            cosine, sine = 1.0 - 2.0 * sine * sine, 2.0 * sine * cosine
        rot_c[z] = cosine
        rot_s[z] = sine

    level = lax.broadcasted_iota(jnp.int32, (NR, LANES), 0)
    blank = jnp.zeros((NR, LANES), jnp.float32)

    def centre_table(i, local):
        parts = []
        for pair in range(ZB // 2):
            terms, hits = [], []
            for z in (2 * pair, 2 * pair + 1):
                base = z * 16 * GAL
                re = [start[pl.ds(base + i, 8, stride=GAL), :]]
                im = [start[pl.ds(base + 8 * GAL + i, 8, stride=GAL), :]]
                cosine = jnp.broadcast_to(rot_c[z, pl.ds(i, 1), :], (8, LANES))
                sine = jnp.broadcast_to(rot_s[z, pl.ds(i, 1), :], (8, LANES))
                twice = cosine + cosine
                re.append(re[0] * cosine + im[0] * sine)
                im.append(im[0] * cosine - re[0] * sine)
                for _ in range(2):
                    re.append(twice * re[-1] - re[-2])
                    im.append(twice * im[-1] - im[-2])
                terms.append(jnp.concatenate(re + im, axis=0).astype(jnp.bfloat16))
                row = jnp.broadcast_to(bins[z, pl.ds(i, 1), :], (NR, LANES))
                hits.append(jnp.where(row == level, 1.0, 0.0))
            onehot = jnp.concatenate(
                [jnp.concatenate([hits[0], blank], axis=1), jnp.concatenate([blank, hits[1]], axis=1)],
                axis=0,
            ).astype(jnp.bfloat16)
            parts.append((jnp.concatenate(terms, axis=1), onehot))
        empty = jnp.zeros((2 * NR, 2 * LANES), jnp.bfloat16)
        spread = jnp.concatenate(
            [
                jnp.concatenate([hit if a == b else empty for b, (_, hit) in enumerate(parts)], axis=1)
                for a in range(ZB // 2)
            ],
            axis=0,
        )
        table = lax.dot_general(
            jnp.concatenate([part for part, _ in parts], axis=1), spread, (((1,), (1,)), ((), ())),
            preferred_element_type=jnp.float32,
        )
        rows = pl.ds(local, NM, stride=HALF)
        grid0[rows, :] = table[:NM, :LANES]
        grid1[rows, :] = jnp.concatenate([table[:NM, LANES:], table[NM:, LANES:]], axis=1)
        grid2[rows, :] = table[NM:, :LANES]

    def table_copy(half, slot):
        return pltpu.make_async_remote_copy(
            src_ref=send.at[half, tile_at(slot)],
            dst_ref=got.at[pl.ds(pl.multiple_of(slot * GAL + half * HALF, HALF), HALF), :],
            send_sem=tab_send.at[half, slot], recv_sem=tab_recv.at[half, slot],
            device_id={"tile": tile_at(slot)}, device_id_type=MESH,
        )

    for half in range(2):
        @pl.loop(0, HALF, unroll=HALF)
        def _(local):
            centre_table(half * HALF + local, local)

        @pl.loop(0, NM, unroll=4)
        def _(n):
            rows = pl.ds(pl.multiple_of(n * HALF, HALF), HALF)
            send[half, n, :, 0:LANES] = grid0[rows, :].astype(jnp.bfloat16)
            send[half, n, :, LANES:2 * LANES] = grid1[rows, :].astype(jnp.bfloat16)
            send[half, n, :, 2 * LANES:] = grid2[rows, :].astype(jnp.bfloat16)

        @pl.loop(0, OWN)
        def _(slot):
            table_copy(half, slot).start()

        got[OWN * GAL + half * HALF:OWN * GAL + (half + 1) * HALF, :] = send[half, me_t]

    lane = lax.broadcasted_iota(jnp.int32, (2, LANES), 1)
    wide_re[...] = jnp.zeros_like(wide_re)
    wide_im[...] = jnp.zeros_like(wide_im)
    group = 8
    for g in range(TILES // group):
        @pl.loop(g * group, min((g + 1) * group, OWN))
        def _(slot):
            for half in range(2):
                table_copy(half, slot).wait_recv()

        block = got[g * group * GAL:(g + 1) * group * GAL, :]
        turned = block.T.astype(jnp.float32)
        scales = []
        for quad in range(group * GAL // LANES):
            first = g * group + quad * (LANES // GAL)
            row = every[first]
            for k in range(1, LANES // GAL):
                row = jnp.where(lane // GAL == k, every[first + k], row)
            scales.append(row)
        scales = jnp.concatenate(scales, axis=1)
        first, second = scales[0:1], scales[1:2]
        real_in = turned[:LEGS]
        imag_in = jnp.concatenate([turned[WIDE - LANES:], turned[LEGS:WIDE - LANES]], axis=0)
        upper_re = (first * real_in - second * imag_in).astype(jnp.bfloat16)
        upper_im = (first * imag_in + second * real_in).astype(jnp.bfloat16)
        wide_re[...] += jnp.dot(upper_re, block, preferred_element_type=jnp.float32)
        wide_im[...] += jnp.dot(upper_im, block, preferred_element_type=jnp.float32)

    scale = float(TILES * GAL) ** -0.5
    low = lax.broadcasted_iota(jnp.int32, (LEGS // 2, LANES), 1) < LANES // 2
    for part in range(2):
        if part == 0:
            whole = wide_re[:, :LANES] + wide_im[:, 2 * LANES:]
            rest = wide_re[:, LANES:2 * LANES] + pltpu.roll(wide_im[:, LANES:2 * LANES], LANES // 2, 1)
        else:
            whole = wide_im[:, :LANES] - wide_re[:, 2 * LANES:]
            rest = wide_im[:, LANES:2 * LANES] - pltpu.roll(wide_re[:, LANES:2 * LANES], LANES // 2, 1)
        block_a[...] = whole * scale
        block_b[...] = rest * scale
        base = part * LEGS * LEGS // LANES
        even_a = block_a[pl.ds(0, LEGS // 2, stride=2), :]
        odd_a = pltpu.roll(block_a[pl.ds(1, LEGS // 2, stride=2), :], LANES // 2, 1)
        even_b = block_b[pl.ds(0, LEGS // 2, stride=2), :]
        odd_b = pltpu.roll(block_b[pl.ds(1, LEGS // 2, stride=2), :], LANES // 2, 1)
        out[pl.ds(base, LEGS // 2, stride=3), :] = even_a
        out[pl.ds(base + 1, LEGS // 2, stride=3), :] = jnp.where(low, even_b, odd_a)
        out[pl.ds(base + 2, LEGS // 2, stride=3), :] = jnp.where(low, odd_a, odd_b)

    @pl.loop(0, OWN)
    def _(slot):
        every_copy(slot).wait_send()
        for half in range(2):
            table_copy(half, slot).wait_send()

    @pl.loop(1, ZB)
    def _(step):
        raw_copy(step, 0, angles_in, phi).wait_send()
        raw_copy(step, 1, bins_in, bins).wait_send()
        near_copy(step).wait_send()


def per_device(shear, weight, partner_tiles, pair_count, pair_bin, pair_angle):
    vmem = pl.BlockSpec(memory_space=pltpu.VMEM)
    anywhere = pl.BlockSpec(memory_space=pl.ANY)
    f32, bf16 = jnp.float32, jnp.bfloat16
    flat = pl.pallas_call(
        kernel,
        out_shape=pltpu.VMEM((2 * LEGS * LEGS // LANES, LANES), f32),
        in_specs=[anywhere] * 6,
        out_specs=vmem,
        scratch_shapes=[
            pltpu.VMEM((1, 2, GAL), f32),
            pltpu.VMEM((1, GAL), f32),
            pltpu.SMEM((1, LANES // GAL), jnp.int32),
            pltpu.SMEM((1, 1), jnp.int32),
            pltpu.VMEM((TILES, 2, LANES), f32),
            pltpu.VMEM((ZB, 2, LANES), f32),
            pltpu.VMEM((ZB, GAL, LANES), f32),
            pltpu.VMEM((ZB, GAL, LANES), jnp.int32),
            pltpu.VMEM((ZB * 16 * GAL, LANES), f32),
            pltpu.VMEM((ZB, GAL, LANES), f32),
            pltpu.VMEM((ZB, GAL, LANES), f32),
            pltpu.VMEM((NM * HALF, LANES), f32),
            pltpu.VMEM((NM * HALF, LANES), f32),
            pltpu.VMEM((NM * HALF, LANES), f32),
            pltpu.VMEM((2, NM, HALF, WIDE), bf16),
            pltpu.VMEM((TILES * GAL, WIDE), bf16),
            pltpu.VMEM((LEGS, WIDE), f32),
            pltpu.VMEM((LEGS, WIDE), f32),
            pltpu.VMEM((LEGS, LANES), f32),
            pltpu.VMEM((LEGS, LANES), f32),
            pltpu.SemaphoreType.DMA((4,)),
            pltpu.SemaphoreType.DMA((2,)),
            pltpu.SemaphoreType.DMA((TILES,)),
            pltpu.SemaphoreType.DMA((TILES,)),
            pltpu.SemaphoreType.DMA((2, ZB)),
            pltpu.SemaphoreType.DMA((2, ZB)),
            pltpu.SemaphoreType.DMA((ZB,)),
            pltpu.SemaphoreType.DMA((ZB,)),
            pltpu.SemaphoreType.DMA((2, TILES)),
            pltpu.SemaphoreType.DMA((2, TILES)),
        ],
        compiler_params=pltpu.CompilerParams(
            collective_id=0, has_side_effects=True, vmem_limit_bytes=60 * 1024 * 1024
        ),
        cost_estimate=pl.CostEstimate(flops=800_000_000, bytes_accessed=2_000_000, transcendentals=0),
        name="shear_triples",
    )(shear, weight, partner_tiles, pair_count.reshape(1, 1), pair_bin, pair_angle)
    return flat.reshape(1, 1, 2 * LEGS * LEGS)


def solution(mesh):
    return jax.shard_map(
        per_device,
        mesh=mesh,
        in_specs=(
            P("zbin", None, "tile"),
            P("zbin", "tile"),
            P("tile", None),
            P("tile"),
            P("zbin", "tile", None),
            P("zbin", "tile", None),
        ),
        out_specs=P("zbin", "tile", None),
        check_vma=False,
    )
```

```python
import jax
import jax.numpy as jnp
from jax import lax
from jax.experimental import pallas as pl
from jax.experimental.pallas import tpu as pltpu
from jax.sharding import PartitionSpec as P

GAL = 32
NM = 32
NR = 24
ZB = 8
TILES = 32
YS = 4
ZS = TILES // YS
FAR = ZS // 2
LANES = 128
HALF = 16
LEGS = ZB * NR
WIDE = 2 * LEGS
WINDOW = 4
PART = WINDOW * YS
TERMS = 2 * PART
MESH = pl.DeviceIdType.MESH


def sine_cosine(phi):
    half = phi * 0.5
    sq = half * half
    sin_h = -2.5052108385e-08
    for coefficient in (2.7557319224e-06, -1.9841269841e-04, 8.3333333333e-03, -1.6666666667e-01):
        sin_h = sin_h * sq + coefficient
    sin_h = half + half * (sq * sin_h)
    cos_h = 2.0876756988e-09
    for coefficient in (-2.7557319224e-07, 2.4801587302e-05, -1.3888888889e-03, 4.1666666667e-02, -0.5):
        cos_h = cos_h * sq + coefficient
    cos_h = 1.0 + sq * cos_h
    return 2.0 * sin_h * cos_h, 1.0 - 2.0 * sin_h * sin_h


def doubled(sine, cosine):
    return 2.0 * sine * cosine, 1.0 - 2.0 * sine * sine


def kernel(
    shear_in, weight_in, partners_in, count_in, bins_in, angles_in, out,
    shear, weight, partners, count, bins_all, bins_out, every, near, phi, bins_got, bins, sines, turns_c, turns_s,
    start, grid0, grid1, grid2, send, got, wide_re, wide_im, block_a, block_b,
    small_sem, own_sem, every_send, every_recv, raw_send, raw_recv, near_send, near_recv, tab_send, tab_recv,
):
    me_t = lax.axis_index("tile")
    me_z = lax.axis_index("zbin")
    at_z, at_y = me_t // YS, me_t % YS

    def tile_at(slot):
        return ((at_z + slot // YS) % ZS) * YS + (at_y + slot % YS) % YS

    def tile_from(slot):
        return ((at_z + ZS - slot // YS) % ZS) * YS + (at_y + YS - slot % YS) % YS

    def far_first(k):
        step = k // YS
        return (ZS // 2 + (step + 1) // 2 * (1 - 2 * (step % 2))) % ZS * YS + (k + 1) % YS

    def bin_at(step):
        return (me_z + step) % ZB

    def rows_of(centre_bin):
        return pl.ds(pl.multiple_of(centre_bin * GAL, GAL), GAL)

    opposite = ((at_z + FAR) % ZS) * YS + at_y

    small = [
        pltpu.make_async_copy(shear_in, shear, small_sem.at[0]),
        pltpu.make_async_copy(weight_in, weight, small_sem.at[1]),
        pltpu.make_async_copy(partners_in, partners, small_sem.at[2]),
        pltpu.make_async_copy(count_in, count, small_sem.at[3]),
    ]
    own_bins = pltpu.make_async_copy(bins_in.at[0], bins_all, own_sem.at[0])
    own_angles = pltpu.make_async_copy(angles_in.at[0, rows_of(me_z)], phi.at[0, me_z], own_sem.at[1])
    for copy in small:
        copy.start()
    own_bins.start()
    own_angles.start()
    barrier = pltpu.get_barrier_semaphore()

    @pl.loop(0, TILES - 1)
    def _(k):
        pl.semaphore_signal(barrier, inc=1, device_id={"tile": tile_at(far_first(k))}, device_id_type=MESH)

    @pl.loop(1, ZB)
    def _(step):
        pl.semaphore_signal(barrier, inc=1, device_id={"tile": opposite, "zbin": bin_at(step)}, device_id_type=MESH)

    @pl.loop(1, ZB)
    def _(step):
        pl.semaphore_signal(barrier, inc=1, device_id={"zbin": bin_at(step)}, device_id_type=MESH)

    for copy in small:
        copy.wait()
    lane = lax.broadcasted_iota(jnp.int32, (1, LANES), 1)
    place = lane // GAL
    wanted = jnp.full((1, LANES), partners[0, 0])
    for slot in range(1, LANES // GAL):
        wanted = jnp.where(place == slot, partners[0, slot], wanted)
    wanted = jnp.where(place < count[0, 0], wanted, -1).astype(jnp.float32)
    scaled = shear[0] * weight[...]
    every[0, 0:2, :] = jnp.concatenate([scaled] * (LANES // GAL), axis=1)
    every[0, 2:3, :] = wanted
    every[0, 3:4, :] = wanted
    own_bins.wait()

    @pl.loop(0, ZB)
    def _(c):
        bins_out[c] = bins_all[rows_of(c), :].astype(jnp.float32).astype(jnp.bfloat16)

    bins_got[0, me_z] = bins_out[me_z]
    pl.semaphore_wait(barrier, TILES - 1 + 2 * (ZB - 1))

    def every_copy(slot):
        return pltpu.make_async_remote_copy(
            src_ref=every.at[0], dst_ref=every.at[slot],
            send_sem=every_send.at[slot], recv_sem=every_recv.at[slot],
            device_id={"tile": tile_at(slot)}, device_id_type=MESH,
        )

    def raw_copies(side, step):
        to = bin_at(step)
        device = {"zbin": to} if side == 0 else {"tile": opposite, "zbin": to}
        pairs = ((angles_in.at[0, rows_of(to)], phi), (bins_out.at[to], bins_got))
        return [
            pltpu.make_async_remote_copy(
                src_ref=source, dst_ref=target.at[side, me_z],
                send_sem=raw_send.at[side, kind, step], recv_sem=raw_recv.at[side, kind, step],
                device_id=device, device_id_type=MESH,
            )
            for kind, (source, target) in enumerate(pairs)
        ]

    def near_copy(step):
        return pltpu.make_async_remote_copy(
            src_ref=near.at[me_z], dst_ref=near.at[me_z],
            send_sem=near_send.at[step], recv_sem=near_recv.at[step],
            device_id={"zbin": bin_at(step)}, device_id_type=MESH,
        )

    @pl.loop(0, TILES - 1)
    def _(k):
        every_copy(far_first(k)).start()

    @pl.loop(1, ZB)
    def _(step):
        for copy in raw_copies(0, step):
            copy.start()

    @pl.loop(0, ZB)
    def _(step):
        for copy in raw_copies(1, step):
            copy.start()

    own_angles.wait()

    @pl.loop(1, TILES)
    def _(slot):
        every_copy(slot).wait_recv()

    picked = [jnp.zeros((2, LANES), jnp.float32) for _ in range(2)]
    asked = [jnp.broadcast_to(every[slot, 2:3, :], (2, LANES)) for slot in (0, FAR * YS)]
    for slot in range(TILES):
        number = tile_from(slot).astype(jnp.float32)
        values = every[slot, 0:2, :]
        for side in range(2):
            picked[side] = picked[side] + jnp.where(asked[side] == number, values, 0.0)
    near[me_z] = jnp.concatenate(picked, axis=0)

    @pl.loop(1, ZB)
    def _(step):
        near_copy(step).start()

    def turns(side):
        @pl.loop(0, ZB)
        def _(z):
            sine, cosine = sine_cosine(phi[side, z])
            phi[side, z] = cosine
            sines[side, z] = sine
            bins[side, z] = bins_got[side, z].astype(jnp.float32)
            two = doubled(sine, cosine)
            four = doubled(*two)
            eight = doubled(*four)
            sixteen = doubled(*eight)
            for half in range(2):
                rows = slice(half * HALF, (half + 1) * HALF)
                group = (at_z + ZS - 1 - half) % ZS
                turn_s, turn_c = jnp.zeros((HALF, LANES)), jnp.ones((HALF, LANES))
                for bit, (step_s, step_c) in ((1, four), (2, eight), (4, sixteen)):
                    on = (group // bit) % 2 == 1
                    step_s = jnp.where(on, step_s[rows], 0.0)
                    step_c = jnp.where(on, step_c[rows], 1.0)
                    turn_s, turn_c = turn_s * step_c + turn_c * step_s, turn_c * step_c - turn_s * step_s
                for k in range(WINDOW):
                    turns_c[side, z, k, rows, :] = turn_c
                    turns_s[side, z, k, rows, :] = turn_s
                    wraps = (group + k + 1) % ZS == 0
                    step_s, step_c = four[0][rows], four[1][rows]
                    turn_s, turn_c = (
                        jnp.where(wraps, 0.0, turn_s * step_c + turn_c * step_s),
                        jnp.where(wraps, 1.0, turn_c * step_c - turn_s * step_s),
                    )

    def starts(side):
        @pl.loop(0, ZB)
        def _(z):
            cosine, sine = phi[side, z], sines[side, z]
            first = jnp.broadcast_to(near[z, 2 * side:2 * side + 1, :], (GAL, LANES))
            second = jnp.broadcast_to(near[z, 2 * side + 1:2 * side + 2, :], (GAL, LANES))
            twice = 2.0 * cosine
            base = pl.multiple_of(z * TERMS * GAL, TERMS * GAL)
            for k in range(WINDOW):
                turn_c, turn_s = turns_c[side, z, k], turns_s[side, z, k]
                old_re = first * turn_c + second * turn_s
                old_im = second * turn_c - first * turn_s
                new_re = old_re * cosine + old_im * sine
                new_im = old_im * cosine - old_re * sine
                for r in range(YS):
                    at = base + (k * YS + r) * GAL
                    start[side, pl.ds(at, GAL), :] = old_re
                    start[side, pl.ds(at + PART * GAL, GAL), :] = old_im
                    old_re, new_re = new_re, twice * new_re - old_re
                    old_im, new_im = new_im, twice * new_im - old_im

    level = lax.broadcasted_iota(jnp.int32, (NR, LANES), 0).astype(jnp.float32)
    blank = jnp.zeros((NR, LANES), jnp.float32)
    empty = jnp.zeros((2 * NR, 2 * LANES), jnp.bfloat16)

    def centre_table(side, i, local):
        terms, spread = [], []
        for pair in range(ZB // 2):
            hits = []
            for z in (2 * pair, 2 * pair + 1):
                rows = pl.ds(z * TERMS * GAL + i, TERMS, stride=GAL)
                terms.append(start[side, rows, :].astype(jnp.bfloat16))
                row = jnp.broadcast_to(bins[side, z, pl.ds(i, 1), :], (NR, LANES))
                hits.append(jnp.where(row == level, 1.0, 0.0))
            onehot = jnp.concatenate(
                [jnp.concatenate([hits[0], blank], axis=1), jnp.concatenate([blank, hits[1]], axis=1)],
                axis=0,
            ).astype(jnp.bfloat16)
            spread.append(
                jnp.concatenate([onehot if other == pair else empty for other in range(ZB // 2)], axis=1)
            )
        table = lax.dot_general(
            jnp.concatenate(terms, axis=1), jnp.concatenate(spread, axis=0), (((1,), (1,)), ((), ())),
            preferred_element_type=jnp.float32,
        )
        rows = pl.ds(local, PART, stride=HALF)
        grid0[rows, :] = table[:PART, :LANES]
        grid1[rows, :] = jnp.concatenate([table[:PART, LANES:], table[PART:, LANES:]], axis=1)
        grid2[rows, :] = table[PART:, :LANES]

    def block_rows(side, half, k, y):
        return ((side * WINDOW + k) * YS + y) * GAL + half * HALF

    def is_own(half, k, y):
        return k == 1 + half and y == 0

    def table_copy(side, half, k, y):
        chunk = 2 * side + half
        to_y = (at_y + y) % YS
        return pltpu.make_async_remote_copy(
            src_ref=send.at[chunk, k * YS + to_y],
            dst_ref=got.at[pl.ds(block_rows(side, half, k, y), HALF), :],
            send_sem=tab_send.at[chunk, k * YS + y], recv_sem=tab_recv.at[chunk, k * YS + y],
            device_id={"tile": ((at_z + ZS + k - 1 - half) % ZS) * YS + to_y}, device_id_type=MESH,
        )

    def tables(side):
        for half in range(2):
            chunk = 2 * side + half

            @pl.loop(0, HALF, unroll=HALF)
            def _(local):
                centre_table(side, half * HALF + local, local)

            @pl.loop(0, PART, unroll=4)
            def _(n):
                rows = pl.ds(pl.multiple_of(n * HALF, HALF), HALF)
                send[chunk, n, :, 0:LANES] = grid0[rows, :].astype(jnp.bfloat16)
                send[chunk, n, :, LANES:2 * LANES] = grid1[rows, :].astype(jnp.bfloat16)
                send[chunk, n, :, 2 * LANES:] = grid2[rows, :].astype(jnp.bfloat16)

            for k in ((3, 0, 2, 1), (0, 3, 1, 2))[half]:
                for y in (2, 1, 3, 0):
                    if is_own(half, k, y):
                        at = block_rows(side, half, k, y)
                        got[at:at + HALF, :] = send[chunk, k * YS + at_y]
                    else:
                        table_copy(side, half, k, y).start()

    @pl.loop(1, ZB)
    def _(step):
        for copy in raw_copies(0, step):
            copy.wait_recv()

    turns(0)

    @pl.loop(1, ZB)
    def _(step):
        near_copy(step).wait_recv()

    starts(0)
    tables(0)

    @pl.loop(0, ZB)
    def _(step):
        for copy in raw_copies(1, step):
            copy.wait_recv()

    turns(1)
    starts(1)
    tables(1)

    wide_re[...] = jnp.zeros_like(wide_re)
    wide_im[...] = jnp.zeros_like(wide_im)
    lane = lax.broadcasted_iota(jnp.int32, (2, LANES), 1)
    span = 2
    for side in range(2):
        for begin in range(0, WINDOW, span):
            scales = []
            for k in range(begin, begin + span):
                row = None
                for y in range(YS):
                    for half in range(2):
                        if not is_own(half, k, y):
                            table_copy(side, half, k, y).wait_recv()
                        source = (k - 1 - half - FAR * side) % ZS * YS + y
                        values = every[source, 0:2, :]
                        row = values if row is None else jnp.where(lane // HALF == 2 * y + half, values, row)
                scales.append(row)
            scales = jnp.concatenate(scales, axis=1)
            at = block_rows(side, 0, begin, 0)
            block = got[at:at + span * LANES, :]
            turned = block.T.astype(jnp.float32)
            first, second = scales[0:1], scales[1:2]
            real_in = turned[:LEGS]
            imag_in = jnp.concatenate([turned[WIDE - LANES:], turned[LEGS:WIDE - LANES]], axis=0)
            upper_re = (first * real_in - second * imag_in).astype(jnp.bfloat16)
            upper_im = (first * imag_in + second * real_in).astype(jnp.bfloat16)
            wide_re[...] += jnp.dot(upper_re, block, preferred_element_type=jnp.float32)
            wide_im[...] += jnp.dot(upper_im, block, preferred_element_type=jnp.float32)

    scale = float(TILES * GAL) ** -0.5
    low = lax.broadcasted_iota(jnp.int32, (LEGS // 2, LANES), 1) < LANES // 2
    for part in range(2):
        if part == 0:
            whole = wide_re[:, :LANES] + wide_im[:, 2 * LANES:]
            rest = wide_re[:, LANES:2 * LANES] + pltpu.roll(wide_im[:, LANES:2 * LANES], LANES // 2, 1)
        else:
            whole = wide_im[:, :LANES] - wide_re[:, 2 * LANES:]
            rest = wide_im[:, LANES:2 * LANES] - pltpu.roll(wide_re[:, LANES:2 * LANES], LANES // 2, 1)
        block_a[...] = whole * scale
        block_b[...] = rest * scale
        base = part * LEGS * LEGS // LANES
        even_a = block_a[pl.ds(0, LEGS // 2, stride=2), :]
        odd_a = pltpu.roll(block_a[pl.ds(1, LEGS // 2, stride=2), :], LANES // 2, 1)
        even_b = block_b[pl.ds(0, LEGS // 2, stride=2), :]
        odd_b = pltpu.roll(block_b[pl.ds(1, LEGS // 2, stride=2), :], LANES // 2, 1)
        out[pl.ds(base, LEGS // 2, stride=3), :] = even_a
        out[pl.ds(base + 1, LEGS // 2, stride=3), :] = jnp.where(low, even_b, odd_a)
        out[pl.ds(base + 2, LEGS // 2, stride=3), :] = jnp.where(low, odd_a, odd_b)

    for side in range(2):
        for half in range(2):
            for k in range(WINDOW):
                for y in range(YS):
                    if not is_own(half, k, y):
                        table_copy(side, half, k, y).wait_send()

    @pl.loop(1, TILES)
    def _(slot):
        every_copy(slot).wait_send()

    @pl.loop(1, ZB)
    def _(step):
        for copy in raw_copies(0, step):
            copy.wait_send()
        near_copy(step).wait_send()

    @pl.loop(0, ZB)
    def _(step):
        for copy in raw_copies(1, step):
            copy.wait_send()


def per_device(shear, weight, partner_tiles, pair_count, pair_bin, pair_angle):
    f32, bf16 = jnp.float32, jnp.bfloat16
    vmem, dma = pltpu.VMEM, pltpu.SemaphoreType.DMA
    flat = pl.pallas_call(
        kernel,
        out_shape=vmem((2 * LEGS * LEGS // LANES, LANES), f32),
        in_specs=[pl.BlockSpec(memory_space=pl.ANY)] * 6,
        out_specs=pl.BlockSpec(memory_space=vmem),
        scratch_shapes=[
            vmem((1, 2, GAL), f32),
            vmem((1, GAL), f32),
            pltpu.SMEM((1, LANES // GAL), jnp.int32),
            pltpu.SMEM((1, 1), jnp.int32),
            vmem((ZB * GAL, LANES), jnp.int32),
            vmem((ZB, GAL, LANES), bf16),
            vmem((TILES, 4, LANES), f32),
            vmem((ZB, 4, LANES), f32),
            vmem((2, ZB, GAL, LANES), f32),
            vmem((2, ZB, GAL, LANES), bf16),
            vmem((2, ZB, GAL, LANES), f32),
            vmem((2, ZB, GAL, LANES), f32),
            vmem((2, ZB, WINDOW, GAL, LANES), f32),
            vmem((2, ZB, WINDOW, GAL, LANES), f32),
            vmem((2, ZB * TERMS * GAL, LANES), f32),
            vmem((PART * HALF, LANES), f32),
            vmem((PART * HALF, LANES), f32),
            vmem((PART * HALF, LANES), f32),
            vmem((4, PART, HALF, WIDE), bf16),
            vmem((TILES * GAL, WIDE), bf16),
            vmem((LEGS, WIDE), f32),
            vmem((LEGS, WIDE), f32),
            vmem((LEGS, LANES), f32),
            vmem((LEGS, LANES), f32),
            dma((4,)),
            dma((2,)),
            dma((TILES,)),
            dma((TILES,)),
            dma((2, 2, ZB)),
            dma((2, 2, ZB)),
            dma((ZB,)),
            dma((ZB,)),
            dma((4, PART)),
            dma((4, PART)),
        ],
        compiler_params=pltpu.CompilerParams(
            collective_id=0, has_side_effects=True, vmem_limit_bytes=60 * 1024 * 1024
        ),
        cost_estimate=pl.CostEstimate(flops=800_000_000, bytes_accessed=2_000_000, transcendentals=0),
        name="shear_triples",
    )(shear, weight, partner_tiles, pair_count.reshape(1, 1), pair_bin, pair_angle)
    return flat.reshape(1, 1, 2 * LEGS * LEGS)


def solution(mesh):
    return jax.shard_map(
        per_device,
        mesh=mesh,
        in_specs=(
            P("zbin", None, "tile"),
            P("zbin", "tile"),
            P("tile", None),
            P("tile"),
            P("zbin", "tile", None),
            P("zbin", "tile", None),
        ),
        out_specs=P("zbin", "tile", None),
        check_vma=False,
    )
```

```python
import jax
import jax.numpy as jnp
from jax import lax
from jax.experimental import pallas as pl
from jax.experimental.pallas import tpu as pltpu
from jax.sharding import PartitionSpec as P

GAL = 32
NM = 32
NR = 24
ZB = 8
TILES = 32
YS = 4
ZS = TILES // YS
FAR = ZS // 2
LANES = 128
HALF = 16
LEGS = ZB * NR
WIDE = 2 * LEGS
WINDOW = 4
PART = WINDOW * YS
TERMS = 2 * PART
CODE = 10430.0
MESH = pl.DeviceIdType.MESH


def sine_cosine(phi):
    half = phi * 0.5
    sq = half * half
    sin_h = -2.5052108385e-08
    for coefficient in (2.7557319224e-06, -1.9841269841e-04, 8.3333333333e-03, -1.6666666667e-01):
        sin_h = sin_h * sq + coefficient
    sin_h = half + half * (sq * sin_h)
    cos_h = 2.0876756988e-09
    for coefficient in (-2.7557319224e-07, 2.4801587302e-05, -1.3888888889e-03, 4.1666666667e-02, -0.5):
        cos_h = cos_h * sq + coefficient
    cos_h = 1.0 + sq * cos_h
    return 2.0 * sin_h * cos_h, 1.0 - 2.0 * sin_h * sin_h


def doubled(sine, cosine):
    return 2.0 * sine * cosine, 1.0 - 2.0 * sine * sine


def kernel(
    shear_in, weight_in, partners_in, count_in, bins_in, angles_in, out,
    shear, weight, partners, count, bins_all, angles_all, coded, every, near, raw, bins, cosines, sines, turns_c, turns_s,
    start, grid0, grid1, grid2, send, got, wide_re, wide_im, block_a, block_b,
    small_sem, own_sem, every_send, every_recv, raw_send, raw_recv, near_send, near_recv, tab_send, tab_recv,
):
    me_t = lax.axis_index("tile")
    me_z = lax.axis_index("zbin")
    at_z, at_y = me_t // YS, me_t % YS
    z_at = [at_z * YS] + [(at_z + step) % ZS * YS for step in range(1, ZS)]
    y_at = [at_y] + [(at_y + step) % YS for step in range(1, YS)]
    bin_at = [me_z] + [(me_z + step) % ZB for step in range(1, ZB)]
    opposite = z_at[FAR] + at_y

    def tile_at(slot):
        return z_at[slot // YS] + y_at[slot % YS]

    def tile_from(slot):
        return z_at[-(slot // YS) % ZS] + y_at[-(slot % YS) % YS]

    def hops(slot):
        return min(slot // YS, ZS - slot // YS) + min(slot % YS, YS - slot % YS)

    far_first = sorted(range(1, TILES), key=lambda slot: -hops(slot))
    steps_far_first = (4, 3, 5, 2, 6, 7, 1)

    def rows_of(centre_bin):
        return pl.ds(pl.multiple_of(centre_bin * GAL, GAL), GAL)

    small = [
        pltpu.make_async_copy(shear_in, shear, small_sem.at[0]),
        pltpu.make_async_copy(weight_in, weight, small_sem.at[1]),
        pltpu.make_async_copy(partners_in, partners, small_sem.at[2]),
        pltpu.make_async_copy(count_in, count, small_sem.at[3]),
    ]
    own = [
        pltpu.make_async_copy(bins_in.at[0], bins_all, own_sem.at[0]),
        pltpu.make_async_copy(angles_in.at[0], angles_all, own_sem.at[1]),
    ]
    for copy in small + own:
        copy.start()
    barrier = pltpu.get_barrier_semaphore()

    def greet(tile, zbin):
        pl.semaphore_signal(barrier, inc=1, device_id=(tile, zbin), device_id_type=MESH)

    for step in steps_far_first:
        greet(opposite, bin_at[step])
    for slot in far_first:
        greet(tile_at(slot), me_z)
    for step in steps_far_first:
        greet(me_t, bin_at[step])

    for copy in small:
        copy.wait()
    lane = lax.broadcasted_iota(jnp.int32, (1, LANES), 1)
    place = lane // GAL
    wanted = jnp.full((1, LANES), partners[0, 0])
    for slot in range(1, LANES // GAL):
        wanted = jnp.where(place == slot, partners[0, slot], wanted)
    wanted = jnp.where(place < count[0, 0], wanted, -1).astype(jnp.float32)
    scaled = shear[0] * weight[...]
    every[0, 0:2, :] = jnp.concatenate([scaled] * (LANES // GAL), axis=1)
    every[0, 2:3, :] = wanted
    every[0, 3:4, :] = wanted
    for copy in own:
        copy.wait()

    @pl.loop(0, ZB)
    def _(c):
        angles = angles_all[rows_of(c), :] * CODE
        angles = (angles + jnp.where(angles < 0.0, -0.5, 0.5)).astype(jnp.int32).astype(jnp.int16)
        numbers = bins_all[rows_of(c), :].astype(jnp.int16)
        for half in range(2):
            coded[c, half, 0] = angles[half * HALF:(half + 1) * HALF]
            coded[c, half, 1] = numbers[half * HALF:(half + 1) * HALF]

    raw[0, me_z] = coded[me_z]
    pl.semaphore_wait(barrier, TILES - 1 + 2 * (ZB - 1))

    def every_copy(slot):
        return pltpu.make_async_remote_copy(
            src_ref=every.at[0], dst_ref=every.at[slot],
            send_sem=every_send.at[slot], recv_sem=every_recv.at[slot],
            device_id=(tile_at(slot), me_z), device_id_type=MESH,
        )

    def raw_copy(step):
        return pltpu.make_async_remote_copy(
            src_ref=coded.at[bin_at[step]], dst_ref=raw.at[0, me_z],
            send_sem=raw_send.at[0, step], recv_sem=raw_recv.at[0, step],
            device_id=(me_t, bin_at[step]), device_id_type=MESH,
        )

    def far_copy(half, step):
        return pltpu.make_async_remote_copy(
            src_ref=coded.at[bin_at[step], half], dst_ref=raw.at[1, me_z, half],
            send_sem=raw_send.at[1 + half, step], recv_sem=raw_recv.at[1 + half, step],
            device_id=(opposite, bin_at[step]), device_id_type=MESH,
        )

    def near_copy(step):
        return pltpu.make_async_remote_copy(
            src_ref=near.at[me_z], dst_ref=near.at[me_z],
            send_sem=near_send.at[step], recv_sem=near_recv.at[step],
            device_id=(me_t, bin_at[step]), device_id_type=MESH,
        )

    for slot in far_first:
        every_copy(slot).start()
    for step in steps_far_first:
        raw_copy(step).start()
    for step in steps_far_first + (0,):
        far_copy(0, step).start()
    for slot in far_first:
        every_copy(slot).wait_recv()

    picked = [jnp.zeros((2, LANES), jnp.float32) for _ in range(2)]
    asked = [jnp.broadcast_to(every[slot, 2:3, :], (2, LANES)) for slot in (0, FAR * YS)]
    for slot in range(TILES):
        number = tile_from(slot).astype(jnp.float32)
        values = every[slot, 0:2, :]
        for side in range(2):
            picked[side] = picked[side] + jnp.where(asked[side] == number, values, 0.0)
    near[me_z] = jnp.concatenate(picked, axis=0)
    for step in steps_far_first:
        near_copy(step).start()
    for step in steps_far_first + (0,):
        far_copy(1, step).start()

    def turns(side, half):
        rows = slice(half * HALF, (half + 1) * HALF)
        group = (at_z + ZS - 1 - half) % ZS

        @pl.loop(0, ZB)
        def _(z):
            angles = raw[side, z, half, 0].astype(jnp.int32).astype(jnp.float32) * (1.0 / CODE)
            bins[side, z, rows, :] = raw[side, z, half, 1].astype(jnp.int32).astype(jnp.float32)
            sine, cosine = sine_cosine(angles)
            cosines[side, z, rows, :] = cosine
            sines[side, z, rows, :] = sine
            four = doubled(*doubled(sine, cosine))
            eight = doubled(*four)
            sixteen = doubled(*eight)
            turn_s, turn_c = jnp.zeros((HALF, LANES)), jnp.ones((HALF, LANES))
            for bit, (step_s, step_c) in ((1, four), (2, eight), (4, sixteen)):
                on = (group // bit) % 2 == 1
                step_s = jnp.where(on, step_s, 0.0)
                step_c = jnp.where(on, step_c, 1.0)
                turn_s, turn_c = turn_s * step_c + turn_c * step_s, turn_c * step_c - turn_s * step_s
            for k in range(WINDOW):
                turns_c[side, z, k, rows, :] = turn_c
                turns_s[side, z, k, rows, :] = turn_s
                wraps = (group + k + 1) % ZS == 0
                step_s, step_c = four
                turn_s, turn_c = (
                    jnp.where(wraps, 0.0, turn_s * step_c + turn_c * step_s),
                    jnp.where(wraps, 1.0, turn_c * step_c - turn_s * step_s),
                )

    def starts(side, half):
        rows = slice(half * HALF, (half + 1) * HALF)

        @pl.loop(0, ZB)
        def _(z):
            cosine, sine = cosines[side, z, rows, :], sines[side, z, rows, :]
            first = jnp.broadcast_to(near[z, 2 * side:2 * side + 1, :], (HALF, LANES))
            second = jnp.broadcast_to(near[z, 2 * side + 1:2 * side + 2, :], (HALF, LANES))
            twice = 2.0 * cosine
            base = pl.multiple_of(z * TERMS * GAL, TERMS * GAL) + half * HALF
            for k in range(WINDOW):
                turn_c, turn_s = turns_c[side, z, k, rows, :], turns_s[side, z, k, rows, :]
                old_re = first * turn_c + second * turn_s
                old_im = second * turn_c - first * turn_s
                new_re = old_re * cosine + old_im * sine
                new_im = old_im * cosine - old_re * sine
                for r in range(YS):
                    at = base + (k * YS + r) * GAL
                    start[side, pl.ds(at, HALF), :] = old_re
                    start[side, pl.ds(at + PART * GAL, HALF), :] = old_im
                    old_re, new_re = new_re, twice * new_re - old_re
                    old_im, new_im = new_im, twice * new_im - old_im

    level = lax.broadcasted_iota(jnp.int32, (NR, LANES), 0).astype(jnp.float32)
    blank = jnp.zeros((NR, LANES), jnp.float32)
    empty = jnp.zeros((2 * NR, 2 * LANES), jnp.bfloat16)

    def centre_table(side, i, local):
        terms, spread = [], []
        for pair in range(ZB // 2):
            hits = []
            for z in (2 * pair, 2 * pair + 1):
                rows = pl.ds(z * TERMS * GAL + i, TERMS, stride=GAL)
                terms.append(start[side, rows, :].astype(jnp.bfloat16))
                row = jnp.broadcast_to(bins[side, z, pl.ds(i, 1), :], (NR, LANES))
                hits.append(jnp.where(row == level, 1.0, 0.0))
            onehot = jnp.concatenate(
                [jnp.concatenate([hits[0], blank], axis=1), jnp.concatenate([blank, hits[1]], axis=1)],
                axis=0,
            ).astype(jnp.bfloat16)
            spread.append(
                jnp.concatenate([onehot if other == pair else empty for other in range(ZB // 2)], axis=1)
            )
        table = lax.dot_general(
            jnp.concatenate(terms, axis=1), jnp.concatenate(spread, axis=0), (((1,), (1,)), ((), ())),
            preferred_element_type=jnp.float32,
        )
        rows = pl.ds(local, PART, stride=HALF)
        grid0[rows, :] = table[:PART, :LANES]
        grid1[rows, :] = jnp.concatenate([table[:PART, LANES:], table[PART:, LANES:]], axis=1)
        grid2[rows, :] = table[PART:, :LANES]

    def block_rows(side, half, k, y):
        return ((side * WINDOW + k) * YS + y) * GAL + half * HALF

    def is_own(half, k, y):
        return k == 1 + half and y == 0

    def table_copy(side, half, k, y):
        chunk = 2 * side + half
        to_y = y_at[y]
        return pltpu.make_async_remote_copy(
            src_ref=send.at[chunk, k * YS + to_y],
            dst_ref=got.at[pl.ds(block_rows(side, half, k, y), HALF), :],
            send_sem=tab_send.at[chunk, k * YS + y], recv_sem=tab_recv.at[chunk, k * YS + y],
            device_id=(z_at[(k - 1 - half) % ZS] + to_y, me_z), device_id_type=MESH,
        )

    def tables(side, half):
        chunk = 2 * side + half

        @pl.loop(0, HALF, unroll=HALF)
        def _(local):
            centre_table(side, half * HALF + local, local)

        @pl.loop(0, PART, unroll=4)
        def _(n):
            rows = pl.ds(pl.multiple_of(n * HALF, HALF), HALF)
            send[chunk, n, :, 0:LANES] = grid0[rows, :].astype(jnp.bfloat16)
            send[chunk, n, :, LANES:2 * LANES] = grid1[rows, :].astype(jnp.bfloat16)
            send[chunk, n, :, 2 * LANES:] = grid2[rows, :].astype(jnp.bfloat16)

        for k in ((3, 0, 2, 1), (0, 3, 1, 2))[half]:
            for y in (2, 1, 3, 0):
                if is_own(half, k, y):
                    at = block_rows(side, half, k, y)
                    got[at:at + HALF, :] = send[chunk, k * YS + at_y]
                else:
                    table_copy(side, half, k, y).start()

    for step in steps_far_first:
        raw_copy(step).wait_recv()
    turns(0, 0)
    turns(0, 1)
    for step in steps_far_first:
        near_copy(step).wait_recv()
    for half in range(2):
        starts(0, half)
        tables(0, half)
    for half in range(2):
        for step in steps_far_first + (0,):
            far_copy(half, step).wait_recv()
        turns(1, half)
        starts(1, half)
        tables(1, half)

    wide_re[...] = jnp.zeros_like(wide_re)
    wide_im[...] = jnp.zeros_like(wide_im)
    lane = lax.broadcasted_iota(jnp.int32, (2, LANES), 1)
    span = 2
    for side in range(2):
        for begin in range(0, WINDOW, span):
            scales = []
            for k in range(begin, begin + span):
                row = None
                for y in range(YS):
                    for half in range(2):
                        if not is_own(half, k, y):
                            table_copy(side, half, k, y).wait_recv()
                        source = (k - 1 - half - FAR * side) % ZS * YS + y
                        values = every[source, 0:2, :]
                        row = values if row is None else jnp.where(lane // HALF == 2 * y + half, values, row)
                scales.append(row)
            scales = jnp.concatenate(scales, axis=1)
            at = block_rows(side, 0, begin, 0)
            block = got[at:at + span * LANES, :]
            turned = block.T.astype(jnp.float32)
            first, second = scales[0:1], scales[1:2]
            real_in = turned[:LEGS]
            imag_in = jnp.concatenate([turned[WIDE - LANES:], turned[LEGS:WIDE - LANES]], axis=0)
            upper_re = (first * real_in - second * imag_in).astype(jnp.bfloat16)
            upper_im = (first * imag_in + second * real_in).astype(jnp.bfloat16)
            wide_re[...] += jnp.dot(upper_re, block, preferred_element_type=jnp.float32)
            wide_im[...] += jnp.dot(upper_im, block, preferred_element_type=jnp.float32)

    scale = float(TILES * GAL) ** -0.5
    low = lax.broadcasted_iota(jnp.int32, (LEGS // 2, LANES), 1) < LANES // 2
    for part in range(2):
        if part == 0:
            whole = wide_re[:, :LANES] + wide_im[:, 2 * LANES:]
            rest = wide_re[:, LANES:2 * LANES] + pltpu.roll(wide_im[:, LANES:2 * LANES], LANES // 2, 1)
        else:
            whole = wide_im[:, :LANES] - wide_re[:, 2 * LANES:]
            rest = wide_im[:, LANES:2 * LANES] - pltpu.roll(wide_re[:, LANES:2 * LANES], LANES // 2, 1)
        block_a[...] = whole * scale
        block_b[...] = rest * scale
        base = part * LEGS * LEGS // LANES
        even_a = block_a[pl.ds(0, LEGS // 2, stride=2), :]
        odd_a = pltpu.roll(block_a[pl.ds(1, LEGS // 2, stride=2), :], LANES // 2, 1)
        even_b = block_b[pl.ds(0, LEGS // 2, stride=2), :]
        odd_b = pltpu.roll(block_b[pl.ds(1, LEGS // 2, stride=2), :], LANES // 2, 1)
        out[pl.ds(base, LEGS // 2, stride=3), :] = even_a
        out[pl.ds(base + 1, LEGS // 2, stride=3), :] = jnp.where(low, even_b, odd_a)
        out[pl.ds(base + 2, LEGS // 2, stride=3), :] = jnp.where(low, odd_a, odd_b)

    for side in range(2):
        for half in range(2):
            for k in range(WINDOW):
                for y in range(YS):
                    if not is_own(half, k, y):
                        table_copy(side, half, k, y).wait_send()

    for slot in far_first:
        every_copy(slot).wait_send()
    for step in steps_far_first:
        raw_copy(step).wait_send()
        near_copy(step).wait_send()
    for step in steps_far_first + (0,):
        for half in range(2):
            far_copy(half, step).wait_send()


def per_device(shear, weight, partner_tiles, pair_count, pair_bin, pair_angle):
    f32, bf16 = jnp.float32, jnp.bfloat16
    vmem, dma = pltpu.VMEM, pltpu.SemaphoreType.DMA
    flat = pl.pallas_call(
        kernel,
        out_shape=vmem((2 * LEGS * LEGS // LANES, LANES), f32),
        in_specs=[pl.BlockSpec(memory_space=pl.ANY)] * 6,
        out_specs=pl.BlockSpec(memory_space=vmem),
        scratch_shapes=[
            vmem((1, 2, GAL), f32),
            vmem((1, GAL), f32),
            pltpu.SMEM((1, LANES // GAL), jnp.int32),
            pltpu.SMEM((1, 1), jnp.int32),
            vmem((ZB * GAL, LANES), jnp.int32),
            vmem((ZB * GAL, LANES), f32),
            vmem((ZB, 2, 2, HALF, LANES), jnp.int16),
            vmem((TILES, 4, LANES), f32),
            vmem((ZB, 4, LANES), f32),
            vmem((2, ZB, 2, 2, HALF, LANES), jnp.int16),
            vmem((2, ZB, GAL, LANES), f32),
            vmem((2, ZB, GAL, LANES), f32),
            vmem((2, ZB, GAL, LANES), f32),
            vmem((2, ZB, WINDOW, GAL, LANES), f32),
            vmem((2, ZB, WINDOW, GAL, LANES), f32),
            vmem((2, ZB * TERMS * GAL, LANES), f32),
            vmem((PART * HALF, LANES), f32),
            vmem((PART * HALF, LANES), f32),
            vmem((PART * HALF, LANES), f32),
            vmem((4, PART, HALF, WIDE), bf16),
            vmem((TILES * GAL, WIDE), bf16),
            vmem((LEGS, WIDE), f32),
            vmem((LEGS, WIDE), f32),
            vmem((LEGS, LANES), f32),
            vmem((LEGS, LANES), f32),
            dma((4,)),
            dma((2,)),
            dma((TILES,)),
            dma((TILES,)),
            dma((3, ZB)),
            dma((3, ZB)),
            dma((ZB,)),
            dma((ZB,)),
            dma((4, PART)),
            dma((4, PART)),
        ],
        compiler_params=pltpu.CompilerParams(
            collective_id=0, has_side_effects=True, vmem_limit_bytes=60 * 1024 * 1024
        ),
        cost_estimate=pl.CostEstimate(flops=800_000_000, bytes_accessed=2_000_000, transcendentals=0),
        name="shear_triples",
    )(shear, weight, partner_tiles, pair_count.reshape(1, 1), pair_bin, pair_angle)
    return flat.reshape(1, 1, 2 * LEGS * LEGS)


def solution(mesh):
    return jax.shard_map(
        per_device,
        mesh=mesh,
        in_specs=(
            P("zbin", None, "tile"),
            P("zbin", "tile"),
            P("tile", None),
            P("tile"),
            P("zbin", "tile", None),
            P("zbin", "tile", None),
        ),
        out_specs=P("zbin", "tile", None),
        check_vma=False,
    )
```

```python
import jax
import jax.numpy as jnp
from jax import lax
from jax.experimental import pallas as pl
from jax.experimental.pallas import tpu as pltpu
from jax.sharding import PartitionSpec as P

GAL = 32
NM = 32
NR = 24
ZB = 8
TILES = 32
YS = 4
ZS = TILES // YS
FAR = ZS // 2
LANES = 128
HALF = 16
LEGS = ZB * NR
WIDE = 2 * LEGS
WINDOW = 4
PART = WINDOW * YS
TERMS = 2 * PART
PITCH = GAL + 4
SPLIT = LANES - 4 * NR
CODE = 10430.0
MESH = pl.DeviceIdType.MESH


def sine_cosine(phi):
    half = phi * 0.5
    sq = half * half
    sin_h = -2.5052108385e-08
    for coefficient in (2.7557319224e-06, -1.9841269841e-04, 8.3333333333e-03, -1.6666666667e-01):
        sin_h = sin_h * sq + coefficient
    sin_h = half + half * (sq * sin_h)
    cos_h = 2.0876756988e-09
    for coefficient in (-2.7557319224e-07, 2.4801587302e-05, -1.3888888889e-03, 4.1666666667e-02, -0.5):
        cos_h = cos_h * sq + coefficient
    cos_h = 1.0 + sq * cos_h
    return 2.0 * sin_h * cos_h, 1.0 - 2.0 * sin_h * sin_h


def doubled(sine, cosine):
    return 2.0 * sine * cosine, 1.0 - 2.0 * sine * sine


def kernel(
    shear_in, weight_in, partners_in, count_in, bins_in, angles_in, out,
    shear, weight, partners, count, bins_all, angles_all, coded, every, near, raw, bins, cosines, sines, turns_c, turns_s,
    start, grid0, grid1, grid2, send, got, wide_re, wide_im, block_a, block_b,
    small_sem, own_sem, every_send, every_recv, raw_send, raw_recv, near_send, near_recv, tab_send, tab_recv,
):
    me_t = lax.axis_index("tile")
    me_z = lax.axis_index("zbin")
    at_z, at_y = me_t // YS, me_t % YS
    z_at = [at_z * YS] + [(at_z + step) % ZS * YS for step in range(1, ZS)]
    y_at = [at_y] + [(at_y + step) % YS for step in range(1, YS)]
    bin_at = [me_z] + [(me_z + step) % ZB for step in range(1, ZB)]
    opposite = z_at[FAR] + at_y

    def tile_at(slot):
        return z_at[slot // YS] + y_at[slot % YS]

    def tile_from(slot):
        return z_at[-(slot // YS) % ZS] + y_at[-(slot % YS) % YS]

    def hops(slot):
        return min(slot // YS, ZS - slot // YS) + min(slot % YS, YS - slot % YS)

    far_first = sorted(range(1, TILES), key=lambda slot: -hops(slot))
    steps_far_first = (4, 3, 5, 2, 6, 7, 1)

    def rows_of(centre_bin):
        return pl.ds(pl.multiple_of(centre_bin * GAL, GAL), GAL)

    small = [
        pltpu.make_async_copy(shear_in, shear, small_sem.at[0]),
        pltpu.make_async_copy(weight_in, weight, small_sem.at[1]),
        pltpu.make_async_copy(partners_in, partners, small_sem.at[2]),
        pltpu.make_async_copy(count_in, count, small_sem.at[3]),
    ]
    own = [
        pltpu.make_async_copy(bins_in.at[0], bins_all, own_sem.at[0]),
        pltpu.make_async_copy(angles_in.at[0], angles_all, own_sem.at[1]),
    ]
    for copy in small + own:
        copy.start()
    barrier = pltpu.get_barrier_semaphore()

    def greet(tile, zbin):
        pl.semaphore_signal(barrier, inc=1, device_id=(tile, zbin), device_id_type=MESH)

    for step in steps_far_first:
        greet(opposite, bin_at[step])
    for slot in far_first:
        greet(tile_at(slot), me_z)
    for step in steps_far_first:
        greet(me_t, bin_at[step])

    for copy in small:
        copy.wait()
    lane = lax.broadcasted_iota(jnp.int32, (1, LANES), 1)
    place = lane // GAL
    wanted = jnp.full((1, LANES), partners[0, 0])
    for slot in range(1, LANES // GAL):
        wanted = jnp.where(place == slot, partners[0, slot], wanted)
    wanted = jnp.where(place < count[0, 0], wanted, -1).astype(jnp.float32)
    scaled = shear[0] * weight[...]
    every[0, 0:2, :] = jnp.concatenate([scaled] * (LANES // GAL), axis=1)
    every[0, 2:3, :] = wanted
    every[0, 3:4, :] = wanted
    for copy in own:
        copy.wait()

    @pl.loop(0, ZB)
    def _(c):
        angles = angles_all[rows_of(c), :] * CODE
        angles = (angles + jnp.where(angles < 0.0, -0.5, 0.5)).astype(jnp.int32).astype(jnp.int16)
        numbers = bins_all[rows_of(c), :].astype(jnp.int16)
        for half in range(2):
            coded[c, half, 0] = angles[half * HALF:(half + 1) * HALF]
            coded[c, half, 1] = numbers[half * HALF:(half + 1) * HALF]

    raw[0, me_z] = coded[me_z]
    pl.semaphore_wait(barrier, TILES - 1 + 2 * (ZB - 1))

    def every_copy(slot):
        return pltpu.make_async_remote_copy(
            src_ref=every.at[0], dst_ref=every.at[slot],
            send_sem=every_send.at[slot], recv_sem=every_recv.at[slot],
            device_id=(tile_at(slot), me_z), device_id_type=MESH,
        )

    def raw_copy(step):
        return pltpu.make_async_remote_copy(
            src_ref=coded.at[bin_at[step]], dst_ref=raw.at[0, me_z],
            send_sem=raw_send.at[0, step], recv_sem=raw_recv.at[0, step],
            device_id=(me_t, bin_at[step]), device_id_type=MESH,
        )

    def far_copy(half, step):
        return pltpu.make_async_remote_copy(
            src_ref=coded.at[bin_at[step], half], dst_ref=raw.at[1, me_z, half],
            send_sem=raw_send.at[1 + half, step], recv_sem=raw_recv.at[1 + half, step],
            device_id=(opposite, bin_at[step]), device_id_type=MESH,
        )

    def near_copy(step):
        return pltpu.make_async_remote_copy(
            src_ref=near.at[me_z], dst_ref=near.at[me_z],
            send_sem=near_send.at[step], recv_sem=near_recv.at[step],
            device_id=(me_t, bin_at[step]), device_id_type=MESH,
        )

    for slot in far_first:
        every_copy(slot).start()
    for step in steps_far_first:
        raw_copy(step).start()
    for step in steps_far_first + (0,):
        far_copy(0, step).start()
    for slot in far_first:
        every_copy(slot).wait_recv()

    picked = [jnp.zeros((2, LANES), jnp.float32) for _ in range(2)]
    asked = [jnp.broadcast_to(every[slot, 2:3, :], (2, LANES)) for slot in (0, FAR * YS)]
    for slot in range(TILES):
        number = tile_from(slot).astype(jnp.float32)
        values = every[slot, 0:2, :]
        for side in range(2):
            picked[side] = picked[side] + jnp.where(asked[side] == number, values, 0.0)
    near[me_z] = jnp.concatenate(picked, axis=0)
    for step in steps_far_first:
        near_copy(step).start()
    for step in steps_far_first + (0,):
        far_copy(1, step).start()

    def turns(side, half):
        rows = slice(half * HALF, (half + 1) * HALF)
        group = (at_z + ZS - 1 - half) % ZS

        @pl.loop(0, ZB)
        def _(z):
            angles = raw[side, z, half, 0].astype(jnp.int32).astype(jnp.float32) * (1.0 / CODE)
            bins[side, z, rows, :] = raw[side, z, half, 1].astype(jnp.int32).astype(jnp.float32)
            sine, cosine = sine_cosine(angles)
            cosines[side, z, rows, :] = cosine
            sines[side, z, rows, :] = sine
            four = doubled(*doubled(sine, cosine))
            eight = doubled(*four)
            sixteen = doubled(*eight)
            turn_s, turn_c = jnp.zeros((HALF, LANES)), jnp.ones((HALF, LANES))
            for bit, (step_s, step_c) in ((1, four), (2, eight), (4, sixteen)):
                on = (group // bit) % 2 == 1
                step_s = jnp.where(on, step_s, 0.0)
                step_c = jnp.where(on, step_c, 1.0)
                turn_s, turn_c = turn_s * step_c + turn_c * step_s, turn_c * step_c - turn_s * step_s
            for k in range(WINDOW):
                turns_c[side, z, k, rows, :] = turn_c
                turns_s[side, z, k, rows, :] = turn_s
                wraps = (group + k + 1) % ZS == 0
                step_s, step_c = four
                turn_s, turn_c = (
                    jnp.where(wraps, 0.0, turn_s * step_c + turn_c * step_s),
                    jnp.where(wraps, 1.0, turn_c * step_c - turn_s * step_s),
                )

    def starts(side, half):
        rows = slice(half * HALF, (half + 1) * HALF)

        @pl.loop(0, ZB, unroll=ZB)
        def _(z):
            cosine, sine = cosines[side, z, rows, :], sines[side, z, rows, :]
            first = jnp.broadcast_to(near[z, 2 * side:2 * side + 1, :], (HALF, LANES))
            second = jnp.broadcast_to(near[z, 2 * side + 1:2 * side + 2, :], (HALF, LANES))
            twice = 2.0 * cosine
            base = z * TERMS * PITCH + half * HALF
            for k in range(WINDOW):
                turn_c, turn_s = turns_c[side, z, k, rows, :], turns_s[side, z, k, rows, :]
                old_re = first * turn_c + second * turn_s
                old_im = second * turn_c - first * turn_s
                new_re = old_re * cosine + old_im * sine
                new_im = old_im * cosine - old_re * sine
                for r in range(YS):
                    at = base + (k * YS + r) * PITCH
                    start[side, pl.ds(at, HALF), :] = old_re
                    start[side, pl.ds(at + PART * PITCH, HALF), :] = old_im
                    old_re, new_re = new_re, twice * new_re - old_re
                    old_im, new_im = new_im, twice * new_im - old_im

    level = lax.broadcasted_iota(jnp.int32, (NR, LANES), 0).astype(jnp.float32)
    lane = lax.broadcasted_iota(jnp.int32, (TERMS, LANES), 1)

    def line(piece, place):
        blank = jnp.zeros_like(piece)
        return jnp.concatenate([piece if at == place else blank for at in range(ZB // 2)], axis=1)

    def product(terms, lines):
        onehots = jnp.concatenate(lines, axis=0).astype(jnp.bfloat16)
        return lax.dot_general(
            jnp.concatenate(terms, axis=1), onehots, (((1,), (1,)), ((), ())), preferred_element_type=jnp.float32
        )

    def centre_table(side, i, local):
        terms, hits = [], []
        for z in range(ZB):
            rows = pl.ds(z * TERMS * PITCH + i, TERMS, stride=PITCH)
            terms.append(start[side, rows, :].astype(jnp.bfloat16))
            row = jnp.broadcast_to(bins[side, z, pl.ds(i, 1), :], (NR, LANES))
            hits.append(jnp.where(row == level, 1.0, 0.0))
        cut = SPLIT - NR
        table0 = product(terms[:4], [line(hits[z], z) for z in range(4)])
        table1 = product(
            terms[4:],
            [
                line(hits[5][cut:], 1), line(hits[6], 2), line(hits[7], 3),
                jnp.zeros((SPLIT, 4 * LANES)), line(hits[4], 0), line(hits[5][:cut], 1),
            ],
        )
        table0 = jnp.concatenate([table0, jnp.zeros((TERMS, SPLIT))], axis=1)
        front = jnp.where(lane < LANES - SPLIT, table0, table1)
        rows = pl.ds(local, PART, stride=HALF)
        grid0[rows, :] = front[:PART]
        grid1[rows, :] = jnp.where(
            lane[:PART] < LANES // 2, table1[:PART], pltpu.roll(table1[PART:], LANES // 2, 1)
        )
        grid2[rows, :] = front[PART:]

    def block_rows(side, half, k, y):
        return ((side * WINDOW + k) * YS + y) * GAL + half * HALF

    def is_own(half, k, y):
        return k == 1 + half and y == 0

    def table_copy(side, half, k, y):
        chunk = 2 * side + half
        to_y = y_at[y]
        return pltpu.make_async_remote_copy(
            src_ref=send.at[chunk, k * YS + to_y],
            dst_ref=got.at[pl.ds(block_rows(side, half, k, y), HALF), :],
            send_sem=tab_send.at[chunk, k * YS + y], recv_sem=tab_recv.at[chunk, k * YS + y],
            device_id=(z_at[(k - 1 - half) % ZS] + to_y, me_z), device_id_type=MESH,
        )

    def tables(side, half):
        chunk = 2 * side + half

        @pl.loop(0, HALF, unroll=HALF)
        def _(local):
            centre_table(side, half * HALF + local, local)

        @pl.loop(0, PART, unroll=PART)
        def _(n):
            rows = pl.ds(pl.multiple_of(n * HALF, HALF), HALF)
            send[chunk, n, :, 0:LANES] = grid0[rows, :].astype(jnp.bfloat16)
            send[chunk, n, :, LANES:2 * LANES] = grid1[rows, :].astype(jnp.bfloat16)
            send[chunk, n, :, 2 * LANES:] = grid2[rows, :].astype(jnp.bfloat16)

        for k in ((3, 0, 2, 1), (0, 3, 1, 2))[half]:
            for y in (2, 1, 3, 0):
                if is_own(half, k, y):
                    at = block_rows(side, half, k, y)
                    got[at:at + HALF, :] = send[chunk, k * YS + at_y]
                else:
                    table_copy(side, half, k, y).start()

    for step in steps_far_first:
        raw_copy(step).wait_recv()
    turns(0, 0)
    turns(0, 1)
    for step in steps_far_first:
        near_copy(step).wait_recv()
    for half in range(2):
        starts(0, half)
        tables(0, half)
    for half in range(2):
        for step in steps_far_first + (0,):
            far_copy(half, step).wait_recv()
        turns(1, half)
        starts(1, half)
        tables(1, half)

    wide_re[...] = jnp.zeros_like(wide_re)
    wide_im[...] = jnp.zeros_like(wide_im)
    lane = lax.broadcasted_iota(jnp.int32, (2, LANES), 1)
    span = 2
    for side in range(2):
        for begin in range(0, WINDOW, span):
            scales = []
            for k in range(begin, begin + span):
                row = None
                for y in range(YS):
                    for half in range(2):
                        if not is_own(half, k, y):
                            table_copy(side, half, k, y).wait_recv()
                        source = (k - 1 - half - FAR * side) % ZS * YS + y
                        values = every[source, 0:2, :]
                        row = values if row is None else jnp.where(lane // HALF == 2 * y + half, values, row)
                scales.append(row)
            scales = jnp.concatenate(scales, axis=1)
            at = block_rows(side, 0, begin, 0)
            block = got[at:at + span * LANES, :]
            turned = block.T.astype(jnp.float32)
            first, second = scales[0:1], scales[1:2]
            real_in = turned[:LEGS]
            imag_in = jnp.concatenate([turned[WIDE - LANES:], turned[LEGS:WIDE - LANES]], axis=0)
            upper_re = (first * real_in - second * imag_in).astype(jnp.bfloat16)
            upper_im = (first * imag_in + second * real_in).astype(jnp.bfloat16)
            wide_re[...] += jnp.dot(upper_re, block, preferred_element_type=jnp.float32)
            wide_im[...] += jnp.dot(upper_im, block, preferred_element_type=jnp.float32)

    scale = float(TILES * GAL) ** -0.5
    low = lax.broadcasted_iota(jnp.int32, (LEGS // 2, LANES), 1) < LANES // 2
    for part in range(2):
        if part == 0:
            whole = wide_re[:, :LANES] + wide_im[:, 2 * LANES:]
            rest = wide_re[:, LANES:2 * LANES] + pltpu.roll(wide_im[:, LANES:2 * LANES], LANES // 2, 1)
        else:
            whole = wide_im[:, :LANES] - wide_re[:, 2 * LANES:]
            rest = wide_im[:, LANES:2 * LANES] - pltpu.roll(wide_re[:, LANES:2 * LANES], LANES // 2, 1)
        block_a[...] = whole * scale
        block_b[...] = rest * scale
        base = part * LEGS * LEGS // LANES
        even_a = block_a[pl.ds(0, LEGS // 2, stride=2), :]
        odd_a = pltpu.roll(block_a[pl.ds(1, LEGS // 2, stride=2), :], LANES // 2, 1)
        even_b = block_b[pl.ds(0, LEGS // 2, stride=2), :]
        odd_b = pltpu.roll(block_b[pl.ds(1, LEGS // 2, stride=2), :], LANES // 2, 1)
        out[pl.ds(base, LEGS // 2, stride=3), :] = even_a
        out[pl.ds(base + 1, LEGS // 2, stride=3), :] = jnp.where(low, even_b, odd_a)
        out[pl.ds(base + 2, LEGS // 2, stride=3), :] = jnp.where(low, odd_a, odd_b)

    for side in range(2):
        for half in range(2):
            for k in range(WINDOW):
                for y in range(YS):
                    if not is_own(half, k, y):
                        table_copy(side, half, k, y).wait_send()

    for slot in far_first:
        every_copy(slot).wait_send()
    for step in steps_far_first:
        raw_copy(step).wait_send()
        near_copy(step).wait_send()
    for step in steps_far_first + (0,):
        for half in range(2):
            far_copy(half, step).wait_send()


def per_device(shear, weight, partner_tiles, pair_count, pair_bin, pair_angle):
    f32, bf16 = jnp.float32, jnp.bfloat16
    vmem, dma = pltpu.VMEM, pltpu.SemaphoreType.DMA
    flat = pl.pallas_call(
        kernel,
        out_shape=vmem((2 * LEGS * LEGS // LANES, LANES), f32),
        in_specs=[pl.BlockSpec(memory_space=pl.ANY)] * 6,
        out_specs=pl.BlockSpec(memory_space=vmem),
        scratch_shapes=[
            vmem((1, 2, GAL), f32),
            vmem((1, GAL), f32),
            pltpu.SMEM((1, LANES // GAL), jnp.int32),
            pltpu.SMEM((1, 1), jnp.int32),
            vmem((ZB * GAL, LANES), jnp.int32),
            vmem((ZB * GAL, LANES), f32),
            vmem((ZB, 2, 2, HALF, LANES), jnp.int16),
            vmem((TILES, 4, LANES), f32),
            vmem((ZB, 4, LANES), f32),
            vmem((2, ZB, 2, 2, HALF, LANES), jnp.int16),
            vmem((2, ZB, GAL, LANES), f32),
            vmem((2, ZB, GAL, LANES), f32),
            vmem((2, ZB, GAL, LANES), f32),
            vmem((2, ZB, WINDOW, GAL, LANES), f32),
            vmem((2, ZB, WINDOW, GAL, LANES), f32),
            vmem((2, ZB * TERMS * PITCH, LANES), f32),
            vmem((PART * HALF, LANES), f32),
            vmem((PART * HALF, LANES), f32),
            vmem((PART * HALF, LANES), f32),
            vmem((4, PART, HALF, WIDE), bf16),
            vmem((TILES * GAL, WIDE), bf16),
            vmem((LEGS, WIDE), f32),
            vmem((LEGS, WIDE), f32),
            vmem((LEGS, LANES), f32),
            vmem((LEGS, LANES), f32),
            dma((4,)),
            dma((2,)),
            dma((TILES,)),
            dma((TILES,)),
            dma((3, ZB)),
            dma((3, ZB)),
            dma((ZB,)),
            dma((ZB,)),
            dma((4, PART)),
            dma((4, PART)),
        ],
        compiler_params=pltpu.CompilerParams(
            collective_id=0, has_side_effects=True, vmem_limit_bytes=60 * 1024 * 1024
        ),
        cost_estimate=pl.CostEstimate(flops=800_000_000, bytes_accessed=2_000_000, transcendentals=0),
        name="shear_triples",
    )(shear, weight, partner_tiles, pair_count.reshape(1, 1), pair_bin, pair_angle)
    return flat.reshape(1, 1, 2 * LEGS * LEGS)


def solution(mesh):
    return jax.shard_map(
        per_device,
        mesh=mesh,
        in_specs=(
            P("zbin", None, "tile"),
            P("zbin", "tile"),
            P("tile", None),
            P("tile"),
            P("zbin", "tile", None),
            P("zbin", "tile", None),
        ),
        out_specs=P("zbin", "tile", None),
        check_vma=False,
    )
```

```python
import jax
import jax.numpy as jnp
from jax import lax
from jax.experimental import pallas as pl
from jax.experimental.pallas import tpu as pltpu
from jax.sharding import PartitionSpec as P

GAL = 32
NM = 32
NR = 24
ZB = 8
TILES = 32
YS = 4
ZS = TILES // YS
FAR = ZS // 2
LANES = 128
HALF = 16
LEGS = ZB * NR
WIDE = 2 * LEGS
WINDOW = 4
PART = WINDOW * YS
TERMS = 2 * PART
PITCH = GAL + 4
SPLIT = LANES - 4 * NR
CODE = 10430.0
MESH = pl.DeviceIdType.MESH


def sine_cosine(phi):
    half = phi * 0.5
    sq = half * half
    sin_h = -2.5052108385e-08
    for coefficient in (2.7557319224e-06, -1.9841269841e-04, 8.3333333333e-03, -1.6666666667e-01):
        sin_h = sin_h * sq + coefficient
    sin_h = half + half * (sq * sin_h)
    cos_h = 2.0876756988e-09
    for coefficient in (-2.7557319224e-07, 2.4801587302e-05, -1.3888888889e-03, 4.1666666667e-02, -0.5):
        cos_h = cos_h * sq + coefficient
    cos_h = 1.0 + sq * cos_h
    return 2.0 * sin_h * cos_h, 1.0 - 2.0 * sin_h * sin_h


def doubled(sine, cosine):
    return 2.0 * sine * cosine, 1.0 - 2.0 * sine * sine


def kernel(
    shear_in, weight_in, partners_in, count_in, bins_in, angles_in, out,
    shear, weight, partners, count, bins_all, angles_all, coded, every, near, raw, bins, cosines, sines, turns_c, turns_s,
    start, grid0, grid1, grid2, send, got, wide_re, wide_im, block_a, block_b,
    small_sem, own_sem, every_send, every_recv, raw_send, raw_recv, near_send, near_recv, tab_send, tab_recv,
):
    me_t = lax.axis_index("tile")
    me_z = lax.axis_index("zbin")
    at_z, at_y = me_t // YS, me_t % YS
    z_at = [at_z * YS] + [(at_z + step) % ZS * YS for step in range(1, ZS)]
    y_at = [at_y] + [(at_y + step) % YS for step in range(1, YS)]
    bin_at = [me_z] + [(me_z + step) % ZB for step in range(1, ZB)]
    opposite = z_at[FAR] + at_y

    def tile_at(slot):
        return z_at[slot // YS] + y_at[slot % YS]

    def tile_from(slot):
        return z_at[-(slot // YS) % ZS] + y_at[-(slot % YS) % YS]

    def hops(slot):
        return min(slot // YS, ZS - slot // YS) + min(slot % YS, YS - slot % YS)

    far_first = sorted(range(1, TILES), key=lambda slot: -hops(slot))
    steps_far_first = (4, 3, 5, 2, 6, 7, 1)

    def rows_of(centre_bin):
        return pl.ds(pl.multiple_of(centre_bin * GAL, GAL), GAL)

    small = [
        pltpu.make_async_copy(shear_in, shear, small_sem.at[0]),
        pltpu.make_async_copy(weight_in, weight, small_sem.at[1]),
        pltpu.make_async_copy(partners_in, partners, small_sem.at[2]),
        pltpu.make_async_copy(count_in, count, small_sem.at[3]),
    ]
    own = [
        pltpu.make_async_copy(bins_in.at[0], bins_all, own_sem.at[0]),
        pltpu.make_async_copy(angles_in.at[0], angles_all, own_sem.at[1]),
    ]
    for copy in small + own:
        copy.start()
    barrier = pltpu.get_barrier_semaphore()

    def greet(tile, zbin):
        pl.semaphore_signal(barrier, inc=1, device_id=(tile, zbin), device_id_type=MESH)

    for step in steps_far_first:
        greet(opposite, bin_at[step])
    for slot in far_first:
        greet(tile_at(slot), me_z)
    for step in steps_far_first:
        greet(me_t, bin_at[step])

    for copy in small:
        copy.wait()
    lane = lax.broadcasted_iota(jnp.int32, (1, LANES), 1)
    place = lane // GAL
    wanted = jnp.full((1, LANES), partners[0, 0])
    for slot in range(1, LANES // GAL):
        wanted = jnp.where(place == slot, partners[0, slot], wanted)
    wanted = jnp.where(place < count[0, 0], wanted, -1).astype(jnp.float32)
    scaled = shear[0] * weight[...]
    every[0, 0:2, :] = jnp.concatenate([scaled] * (LANES // GAL), axis=1)
    every[0, 2:3, :] = wanted
    every[0, 3:4, :] = wanted
    for copy in own:
        copy.wait()

    @pl.loop(0, ZB)
    def _(c):
        angles = angles_all[rows_of(c), :] * CODE
        angles = (angles + jnp.where(angles < 0.0, -0.5, 0.5)).astype(jnp.int32).astype(jnp.int16)
        numbers = bins_all[rows_of(c), :].astype(jnp.int16)
        for half in range(2):
            coded[c, half, 0] = angles[half * HALF:(half + 1) * HALF]
            coded[c, half, 1] = numbers[half * HALF:(half + 1) * HALF]

    raw[0, me_z] = coded[me_z]
    pl.semaphore_wait(barrier, TILES - 1 + 2 * (ZB - 1))

    def every_copy(slot):
        return pltpu.make_async_remote_copy(
            src_ref=every.at[0], dst_ref=every.at[slot],
            send_sem=every_send.at[slot], recv_sem=every_recv.at[slot],
            device_id=(tile_at(slot), me_z), device_id_type=MESH,
        )

    def raw_copy(step):
        return pltpu.make_async_remote_copy(
            src_ref=coded.at[bin_at[step]], dst_ref=raw.at[0, me_z],
            send_sem=raw_send.at[0, step], recv_sem=raw_recv.at[0, step],
            device_id=(me_t, bin_at[step]), device_id_type=MESH,
        )

    def far_copy(half, step):
        return pltpu.make_async_remote_copy(
            src_ref=coded.at[bin_at[step], half], dst_ref=raw.at[1, me_z, half],
            send_sem=raw_send.at[1 + half, step], recv_sem=raw_recv.at[1 + half, step],
            device_id=(opposite, bin_at[step]), device_id_type=MESH,
        )

    def near_copy(step):
        return pltpu.make_async_remote_copy(
            src_ref=near.at[me_z], dst_ref=near.at[me_z],
            send_sem=near_send.at[step], recv_sem=near_recv.at[step],
            device_id=(me_t, bin_at[step]), device_id_type=MESH,
        )

    for slot in far_first:
        every_copy(slot).start()
    for step in steps_far_first:
        raw_copy(step).start()
    for step in steps_far_first + (0,):
        far_copy(0, step).start()
    for slot in far_first:
        every_copy(slot).wait_recv()

    picked = [jnp.zeros((2, LANES), jnp.float32) for _ in range(2)]
    asked = [jnp.broadcast_to(every[slot, 2:3, :], (2, LANES)) for slot in (0, FAR * YS)]
    for slot in range(TILES):
        number = tile_from(slot).astype(jnp.float32)
        values = every[slot, 0:2, :]
        for side in range(2):
            picked[side] = picked[side] + jnp.where(asked[side] == number, values, 0.0)
    near[me_z] = jnp.concatenate(picked, axis=0)
    for step in steps_far_first:
        near_copy(step).start()
    for step in steps_far_first + (0,):
        far_copy(1, step).start()

    def turns(side, half):
        rows = slice(half * HALF, (half + 1) * HALF)
        group = (at_z + ZS - 1 - half) % ZS

        @pl.loop(0, ZB)
        def _(z):
            angles = raw[side, z, half, 0].astype(jnp.int32).astype(jnp.float32) * (1.0 / CODE)
            bins[side, z, rows, :] = raw[side, z, half, 1].astype(jnp.int32).astype(jnp.float32)
            sine, cosine = sine_cosine(angles)
            cosines[side, z, rows, :] = cosine
            sines[side, z, rows, :] = sine
            four = doubled(*doubled(sine, cosine))
            eight = doubled(*four)
            sixteen = doubled(*eight)
            turn_s, turn_c = jnp.zeros((HALF, LANES)), jnp.ones((HALF, LANES))
            for bit, (step_s, step_c) in ((1, four), (2, eight), (4, sixteen)):
                on = (group // bit) % 2 == 1
                step_s = jnp.where(on, step_s, 0.0)
                step_c = jnp.where(on, step_c, 1.0)
                turn_s, turn_c = turn_s * step_c + turn_c * step_s, turn_c * step_c - turn_s * step_s
            for k in range(WINDOW):
                turns_c[side, z, k, rows, :] = turn_c
                turns_s[side, z, k, rows, :] = turn_s
                wraps = (group + k + 1) % ZS == 0
                step_s, step_c = four
                turn_s, turn_c = (
                    jnp.where(wraps, 0.0, turn_s * step_c + turn_c * step_s),
                    jnp.where(wraps, 1.0, turn_c * step_c - turn_s * step_s),
                )

    def starts(side, half):
        rows = slice(half * HALF, (half + 1) * HALF)

        @pl.loop(0, ZB, unroll=ZB)
        def _(z):
            cosine, sine = cosines[side, z, rows, :], sines[side, z, rows, :]
            first = jnp.broadcast_to(near[z, 2 * side:2 * side + 1, :], (HALF, LANES))
            second = jnp.broadcast_to(near[z, 2 * side + 1:2 * side + 2, :], (HALF, LANES))
            twice = 2.0 * cosine
            base = z * TERMS * PITCH + half * HALF
            for k in range(WINDOW):
                turn_c, turn_s = turns_c[side, z, k, rows, :], turns_s[side, z, k, rows, :]
                old_re = first * turn_c + second * turn_s
                old_im = second * turn_c - first * turn_s
                new_re = old_re * cosine + old_im * sine
                new_im = old_im * cosine - old_re * sine
                for r in range(YS):
                    at = base + (k * YS + r) * PITCH
                    start[side, pl.ds(at, HALF), :] = old_re
                    start[side, pl.ds(at + PART * PITCH, HALF), :] = old_im
                    old_re, new_re = new_re, twice * new_re - old_re
                    old_im, new_im = new_im, twice * new_im - old_im

    level = lax.broadcasted_iota(jnp.int32, (NR, LANES), 0).astype(jnp.float32)
    lane = lax.broadcasted_iota(jnp.int32, (TERMS, LANES), 1)

    def line(piece, place):
        blank = jnp.zeros_like(piece)
        return jnp.concatenate([piece if at == place else blank for at in range(ZB // 2)], axis=1)

    def product(terms, lines):
        onehots = jnp.concatenate(lines, axis=0).astype(jnp.bfloat16)
        return lax.dot_general(
            jnp.concatenate(terms, axis=1), onehots, (((1,), (1,)), ((), ())), preferred_element_type=jnp.float32
        )

    def centre_table(side, i, local):
        terms, hits = [], []
        for z in range(ZB):
            rows = pl.ds(z * TERMS * PITCH + i, TERMS, stride=PITCH)
            terms.append(start[side, rows, :].astype(jnp.bfloat16))
            row = jnp.broadcast_to(bins[side, z, pl.ds(i, 1), :], (NR, LANES))
            hits.append(jnp.where(row == level, 1.0, 0.0))
        cut = SPLIT - NR
        table0 = product(terms[:4], [line(hits[z], z) for z in range(4)])
        table1 = product(
            terms[4:],
            [
                line(hits[5][cut:], 1), line(hits[6], 2), line(hits[7], 3),
                jnp.zeros((SPLIT, 4 * LANES)), line(hits[4], 0), line(hits[5][:cut], 1),
            ],
        )
        table0 = jnp.concatenate([table0, jnp.zeros((TERMS, SPLIT))], axis=1)
        front = jnp.where(lane < LANES - SPLIT, table0, table1)
        rows = pl.ds(local, PART, stride=HALF)
        grid0[rows, :] = front[:PART]
        grid1[rows, :] = jnp.where(
            lane[:PART] < LANES // 2, table1[:PART], pltpu.roll(table1[PART:], LANES // 2, 1)
        )
        grid2[rows, :] = front[PART:]

    def block_rows(side, half, k, y):
        return ((side * WINDOW + k) * YS + y) * GAL + half * HALF

    def is_own(half, k, y):
        return k == 1 + half and y == 0

    def table_copy(side, half, k, y):
        chunk = 2 * side + half
        to_y = y_at[y]
        return pltpu.make_async_remote_copy(
            src_ref=send.at[chunk, k * YS + to_y],
            dst_ref=got.at[pl.ds(block_rows(side, half, k, y), HALF), :],
            send_sem=tab_send.at[chunk, k * YS + y], recv_sem=tab_recv.at[chunk, k * YS + y],
            device_id=(z_at[(k - 1 - half) % ZS] + to_y, me_z), device_id_type=MESH,
        )

    def tables(side, half):
        chunk = 2 * side + half

        @pl.loop(0, HALF, unroll=HALF)
        def _(local):
            centre_table(side, half * HALF + local, local)

        @pl.loop(0, PART, unroll=PART)
        def _(n):
            rows = pl.ds(pl.multiple_of(n * HALF, HALF), HALF)
            send[chunk, n, :, 0:LANES] = grid0[rows, :].astype(jnp.bfloat16)
            send[chunk, n, :, LANES:2 * LANES] = grid1[rows, :].astype(jnp.bfloat16)
            send[chunk, n, :, 2 * LANES:] = grid2[rows, :].astype(jnp.bfloat16)

        for k in ((3, 0, 2, 1), (0, 3, 1, 2))[half]:
            for y in (2, 1, 3, 0):
                if is_own(half, k, y):
                    at = block_rows(side, half, k, y)
                    got[at:at + HALF, :] = send[chunk, k * YS + at_y]
                else:
                    table_copy(side, half, k, y).start()

    for step in steps_far_first:
        raw_copy(step).wait_recv()
    turns(0, 0)
    turns(0, 1)
    for step in steps_far_first:
        near_copy(step).wait_recv()
    for half in range(2):
        starts(0, half)
        tables(0, half)
    for half in range(2):
        for step in steps_far_first + (0,):
            far_copy(half, step).wait_recv()
        turns(1, half)
        starts(1, half)
        tables(1, half)

    def sent(chunks):
        for side, half in chunks:
            for k in range(WINDOW):
                for y in range(YS):
                    if not is_own(half, k, y):
                        table_copy(side, half, k, y).wait_send()

    for slot in far_first:
        every_copy(slot).wait_send()
    for step in steps_far_first:
        raw_copy(step).wait_send()
        near_copy(step).wait_send()
    for step in steps_far_first + (0,):
        for half in range(2):
            far_copy(half, step).wait_send()

    wide_re[...] = jnp.zeros_like(wide_re)
    wide_im[...] = jnp.zeros_like(wide_im)
    lane = lax.broadcasted_iota(jnp.int32, (2, LANES), 1)
    span = 2
    for side in range(2):
        for begin in range(0, WINDOW, span):
            if (side, begin) == (1, 0):
                sent([(0, 0), (0, 1)])
            if (side, begin) == (1, span):
                sent([(1, 0), (1, 1)])
            scales = []
            for k in range(begin, begin + span):
                row = None
                for y in range(YS):
                    for half in range(2):
                        if not is_own(half, k, y):
                            table_copy(side, half, k, y).wait_recv()
                        source = (k - 1 - half - FAR * side) % ZS * YS + y
                        values = every[source, 0:2, :]
                        row = values if row is None else jnp.where(lane // HALF == 2 * y + half, values, row)
                scales.append(row)
            scales = jnp.concatenate(scales, axis=1)
            at = block_rows(side, 0, begin, 0)
            block = got[at:at + span * LANES, :]
            turned = block.T.astype(jnp.float32)
            first, second = scales[0:1], scales[1:2]
            real_in = turned[:LEGS]
            imag_in = jnp.concatenate([turned[WIDE - LANES:], turned[LEGS:WIDE - LANES]], axis=0)
            upper_re = (first * real_in - second * imag_in).astype(jnp.bfloat16)
            upper_im = (first * imag_in + second * real_in).astype(jnp.bfloat16)
            wide_re[...] += jnp.dot(upper_re, block, preferred_element_type=jnp.float32)
            wide_im[...] += jnp.dot(upper_im, block, preferred_element_type=jnp.float32)

    scale = float(TILES * GAL) ** -0.5
    low = lax.broadcasted_iota(jnp.int32, (LEGS // 2, LANES), 1) < LANES // 2
    for part in range(2):
        if part == 0:
            whole = wide_re[:, :LANES] + wide_im[:, 2 * LANES:]
            rest = wide_re[:, LANES:2 * LANES] + pltpu.roll(wide_im[:, LANES:2 * LANES], LANES // 2, 1)
        else:
            whole = wide_im[:, :LANES] - wide_re[:, 2 * LANES:]
            rest = wide_im[:, LANES:2 * LANES] - pltpu.roll(wide_re[:, LANES:2 * LANES], LANES // 2, 1)
        block_a[...] = whole * scale
        block_b[...] = rest * scale
        base = part * LEGS * LEGS // LANES
        even_a = block_a[pl.ds(0, LEGS // 2, stride=2), :]
        odd_a = pltpu.roll(block_a[pl.ds(1, LEGS // 2, stride=2), :], LANES // 2, 1)
        even_b = block_b[pl.ds(0, LEGS // 2, stride=2), :]
        odd_b = pltpu.roll(block_b[pl.ds(1, LEGS // 2, stride=2), :], LANES // 2, 1)
        out[pl.ds(base, LEGS // 2, stride=3), :] = even_a
        out[pl.ds(base + 1, LEGS // 2, stride=3), :] = jnp.where(low, even_b, odd_a)
        out[pl.ds(base + 2, LEGS // 2, stride=3), :] = jnp.where(low, odd_a, odd_b)


def per_device(shear, weight, partner_tiles, pair_count, pair_bin, pair_angle):
    f32, bf16 = jnp.float32, jnp.bfloat16
    vmem, dma = pltpu.VMEM, pltpu.SemaphoreType.DMA
    flat = pl.pallas_call(
        kernel,
        out_shape=vmem((2 * LEGS * LEGS // LANES, LANES), f32),
        in_specs=[pl.BlockSpec(memory_space=pl.ANY)] * 6,
        out_specs=pl.BlockSpec(memory_space=vmem),
        scratch_shapes=[
            vmem((1, 2, GAL), f32),
            vmem((1, GAL), f32),
            pltpu.SMEM((1, LANES // GAL), jnp.int32),
            pltpu.SMEM((1, 1), jnp.int32),
            vmem((ZB * GAL, LANES), jnp.int32),
            vmem((ZB * GAL, LANES), f32),
            vmem((ZB, 2, 2, HALF, LANES), jnp.int16),
            vmem((TILES, 4, LANES), f32),
            vmem((ZB, 4, LANES), f32),
            vmem((2, ZB, 2, 2, HALF, LANES), jnp.int16),
            vmem((2, ZB, GAL, LANES), f32),
            vmem((2, ZB, GAL, LANES), f32),
            vmem((2, ZB, GAL, LANES), f32),
            vmem((2, ZB, WINDOW, GAL, LANES), f32),
            vmem((2, ZB, WINDOW, GAL, LANES), f32),
            vmem((2, ZB * TERMS * PITCH, LANES), f32),
            vmem((PART * HALF, LANES), f32),
            vmem((PART * HALF, LANES), f32),
            vmem((PART * HALF, LANES), f32),
            vmem((4, PART, HALF, WIDE), bf16),
            vmem((TILES * GAL, WIDE), bf16),
            vmem((LEGS, WIDE), f32),
            vmem((LEGS, WIDE), f32),
            vmem((LEGS, LANES), f32),
            vmem((LEGS, LANES), f32),
            dma((4,)),
            dma((2,)),
            dma((TILES,)),
            dma((TILES,)),
            dma((3, ZB)),
            dma((3, ZB)),
            dma((ZB,)),
            dma((ZB,)),
            dma((4, PART)),
            dma((4, PART)),
        ],
        compiler_params=pltpu.CompilerParams(
            collective_id=0, has_side_effects=True, vmem_limit_bytes=60 * 1024 * 1024
        ),
        cost_estimate=pl.CostEstimate(flops=800_000_000, bytes_accessed=2_000_000, transcendentals=0),
        name="shear_triples",
    )(shear, weight, partner_tiles, pair_count.reshape(1, 1), pair_bin, pair_angle)
    return flat.reshape(1, 1, 2 * LEGS * LEGS)


def solution(mesh):
    return jax.shard_map(
        per_device,
        mesh=mesh,
        in_specs=(
            P("zbin", None, "tile"),
            P("zbin", "tile"),
            P("tile", None),
            P("tile"),
            P("zbin", "tile", None),
            P("zbin", "tile", None),
        ),
        out_specs=P("zbin", "tile", None),
        check_vma=False,
    )
```
